32 devices in a mesh: tm: 4 (over x, core), chan: 8 (over z, y).
Axes of the slice: x: 2, y: 2, z: 4, core: 2. Of those that a mesh axis runs over, the one named last changes fastest.
Arguments:
- voltages: float32 [512, 262144], P('chan', 'tm'), may hold values from -6 to 6
- fir_taps: float32 [4, 2048], replicated, may hold values from -3 to 3
Outputs:
- visibilities: float32 [1024, 2, 512, 512], P(('tm', 'chan'))
The draws below stay inside these ranges and needn't reach their ends.
All inputs are finite; a program needn't handle non-finite values.
Results may differ from the reference program's by a relative error of at most 0.00009.
Values sent between devices are 32-bit elements; how exact they have to be, the bound alone decides.
No kernel may reach another device: no remote copies, remote signals or barrier semaphores. Data moves between devices by JAX's collectives and lax.ppermute only.
A program may use at most 192 MiB of HBM per device.

```python
import jax
import jax.numpy as jnp
from jax import lax

INPUTS = 512
CHANNELS = 1024
TAPS = 4
FRAME = 2048
SPECTRA = 128
SAMPLES = 262144


def block_levels(stream_key, shape, pieces, least, largest):
    gain = 1.0
    for position, parts in pieces:
        draws = jax.random.uniform(jax.random.fold_in(jax.random.fold_in(stream_key, 6), position), (parts,), jnp.float32, least / len(pieces), largest / len(pieces))
        gain = gain * jnp.repeat(jnp.exp(draws), shape[position] // parts).reshape((-1,) + (1,) * (len(shape) - 1 - position))
    return gain


def scatter_about(own_key, extent, width, reach, split=(), held_as=jnp.bfloat16):
    gain = block_levels(own_key, extent, split, -0.22, 0.18) if split else 1.0
    drawn = jax.random.normal(own_key, extent, jnp.float32) * width * gain
    return jnp.minimum(jnp.maximum(drawn, -reach), reach).astype(held_as)


def setup_inputs(seed: int = 0) -> dict:
    splits = jax.random.split(jax.random.key(seed), 3)
    voltages = scatter_about(splits[0], (INPUTS, SAMPLES), 1.0, 6.0, ((0, 8), (1, 4)), jnp.float32)
    fir_taps = scatter_about(splits[1], (TAPS, FRAME), TAPS ** -0.5, 3.0, (), jnp.float32)
    return {"voltages": voltages, "fir_taps": fir_taps}


def correlate_one(owned):
    stacked = jnp.concatenate([owned[0], owned[1]], axis=1)
    turned = jnp.concatenate([owned[1], -owned[0]], axis=1)
    both = jnp.concatenate([stacked, turned], axis=0)
    gram = jnp.dot(both, stacked.T, precision=lax.Precision.HIGHEST) * (1.0 / SPECTRA)
    return gram.reshape(2, INPUTS, INPUTS)

def reference(voltages, fir_taps):
    frames = voltages.reshape(INPUTS, SPECTRA, FRAME)
    padded = jnp.concatenate([jnp.zeros((INPUTS, TAPS - 1, FRAME), jnp.float32), frames], axis=1)
    filtered = jnp.zeros((INPUTS, SPECTRA, FRAME), jnp.float32)
    for tap in range(TAPS):
        start = TAPS - 1 - tap
        filtered = filtered + fir_taps[tap] * padded[:, start:start + SPECTRA, :]
    spectrum = jnp.fft.rfft(filtered, axis=2)[:, :, :CHANNELS]
    scale = 1.0 / jnp.sqrt(jnp.float32(FRAME))
    real_part = (jnp.real(spectrum) * scale).astype(jnp.float32)
    imag_part = (jnp.imag(spectrum) * scale).astype(jnp.float32)
    stacked = jnp.stack([real_part, imag_part], axis=0)
    per_channel = jnp.transpose(stacked, (3, 0, 1, 2))
    return lax.map(correlate_one, per_channel)
```

```python
import functools

import jax
import jax.numpy as jnp
import numpy as np
from jax import lax
from jax.experimental import pallas as pl
from jax.experimental.pallas import tpu as pltpu
from jax.sharding import PartitionSpec as P

LANES = 128
AXES = ("tm", "chan")
NT = (((1,), (1,)), ((), ()))
NN = (((1,), (0,)), ((), ()))


def params(mib):
    return pltpu.CompilerParams(vmem_limit_bytes=mib << 20)


def halves(value):
    high = value.astype(jnp.bfloat16)
    low = (value - high.astype(jnp.float32)).astype(jnp.bfloat16)
    return high, low


def passed_along(value, axis, steps):
    count = lax.axis_size(axis)
    first, last = (max(0, -steps), min(count, count - steps))
    return lax.ppermute(value, axis, [(source, source + steps) for source in range(first, last)])


def filter_kernel(blocks, groups, taps, volt_ref, halo_ref, fir_ref, high_ref, low_ref):
    frame = fir_ref.shape[1]
    edge = taps - 1

    def put(spec, terms):
        total = terms[0] * fir_ref[0:1, :]
        for tap in range(1, taps):
            total = total + terms[tap] * fir_ref[tap : tap + 1, :]
        high, low = halves(total)
        at = (lax.rem(spec, blocks), lax.div(spec, blocks))
        high_ref[at] = high
        low_ref[at] = low

    def old(spec):
        if spec < 0:
            return halo_ref[:, (spec + edge) * frame : (spec + edge + 1) * frame]
        return volt_ref[:, spec * frame : (spec + 1) * frame]

    for spec in range(edge):
        put(spec, [old(spec - tap) for tap in range(taps)])

    def step(spec, carry):
        put(
            spec,
            [
                volt_ref[:, pl.ds(pl.multiple_of((spec - tap) * frame, frame), frame)]
                for tap in range(taps)
            ],
        )
        return carry

    lax.fori_loop(edge, blocks * groups, step, 0)


def filtered_parts(voltages, halo, fir_taps, blocks, groups):
    inputs, samples = voltages.shape
    taps, frame = fir_taps.shape
    rows = 16
    shape = jax.ShapeDtypeStruct((blocks, groups, inputs, frame), jnp.bfloat16)
    out_spec = pl.BlockSpec((blocks, groups, rows, frame), lambda g: (0, 0, g, 0))
    high, low = pl.pallas_call(
        functools.partial(filter_kernel, blocks, groups, taps),
        grid=(inputs // rows,),
        in_specs=[
            pl.BlockSpec((rows, samples), lambda g: (g, 0)),
            pl.BlockSpec((rows, halo.shape[1]), lambda g: (g, 0)),
            pl.BlockSpec((taps, frame), lambda g: (0, 0)),
        ],
        out_specs=[out_spec, out_spec],
        out_shape=[shape, shape],
        compiler_params=params(40),
        cost_estimate=pl.CostEstimate(
            flops=8 * inputs * samples, bytes_accessed=8 * inputs * samples, transcendentals=0
        ),
        name="polyphase_filter",
    )(voltages, halo, fir_taps)
    rows_all = blocks * groups * inputs
    return high.reshape(rows_all, frame), low.reshape(rows_all, frame)


def dft_kernel(owners, per, outer_ref, first_ref, second_ref, high_ref, low_ref, out_ref, th_ref, tl_ref):
    many = max(1, 16 // per)
    frame = high_ref.shape[1]

    @pl.when(pl.program_id(0) == 0)
    def _():
        def rows(step, carry):
            parts = []
            for extra in range(many):
                owner = step * many + extra
                cosine = outer_ref[0, pl.ds(owner, 1), :]
                sine = outer_ref[1, pl.ds(owner, 1), :]
                parts.append(first_ref[...] * cosine + second_ref[...] * sine)
            value = parts[0] if many == 1 else jnp.concatenate(parts, axis=0)
            high, low = halves(value)
            at = pl.ds(pl.multiple_of(step * many * per, many * per), many * per)
            th_ref[at, :] = high
            tl_ref[at, :] = low
            return carry

        lax.fori_loop(0, owners // many, rows, 0)

    dot = functools.partial(lax.dot_general, dimension_numbers=NT, preferred_element_type=jnp.float32)
    total = dot(th_ref[...], high_ref[...])
    total = total + dot(th_ref[...], low_ref[...])
    total = total + dot(tl_ref[...], high_ref[...])
    for block in range(out_ref.shape[1]):
        part = total[:, block * LANES : (block + 1) * LANES]
        out_ref[:, block] = part.reshape(owners, per, LANES)


def dft_chunk(outer, first, second, high, low, owners, blocks):
    per, frame = first.shape
    wide = 2
    rows = wide * LANES
    const = lambda b: (0, 0)
    return pl.pallas_call(
        functools.partial(dft_kernel, owners, per),
        grid=(blocks // wide,),
        in_specs=[
            pl.BlockSpec((2, owners, frame), lambda b: (0, 0, 0)),
            pl.BlockSpec((per, frame), const),
            pl.BlockSpec((per, frame), const),
            pl.BlockSpec((rows, frame), lambda b: (b, 0)),
            pl.BlockSpec((rows, frame), lambda b: (b, 0)),
        ],
        out_specs=pl.BlockSpec((owners, wide, per, LANES), lambda b: (0, b, 0, 0)),
        out_shape=jax.ShapeDtypeStruct((owners, blocks, per, LANES), jnp.float32),
        scratch_shapes=[
            pltpu.VMEM((owners * per, frame), jnp.bfloat16),
            pltpu.VMEM((owners * per, frame), jnp.bfloat16),
        ],
        compiler_params=params(40),
        cost_estimate=pl.CostEstimate(
            flops=6 * owners * per * frame * blocks * LANES,
            bytes_accessed=4 * blocks * LANES * frame + 4 * owners * blocks * per * LANES,
            transcendentals=0,
        ),
        name="dft_chunk",
    )(outer, first, second, high, low)


def correlate_kernel(sizes, scale, got_ref, *rest):
    tm_count, chan_count, blocks, per, inputs = sizes
    out_ref = rest[-1]
    channel = pl.program_id(0)
    groups = LANES // inputs
    channels = per // 2
    lane_group = lax.broadcasted_iota(jnp.int32, (blocks, LANES), 1) // inputs

    def piece(time, chan, part):
        start = (time * chan_count + chan) * blocks * per + part * channels + channel
        return got_ref[pl.ds(start, blocks, stride=per), :]

    def tile(time, part, column):
        held = [piece(time, column * groups + place, part) for place in range(groups)]
        made = []
        for group in range(groups):
            total = None
            for place in range(groups):
                turn = (place - group) * inputs % LANES
                value = pltpu.roll(held[place], turn, 1) if turn else held[place]
                total = value if total is None else jnp.where(lane_group == place, value, total)
            made.append(total)
        return jnp.concatenate(made, axis=0)

    def plane(part):
        columns = []
        for column in range(chan_count // groups):
            columns.append(
                jnp.concatenate([tile(time, part, column) for time in range(tm_count)], axis=0)
            )
        return jnp.concatenate(columns, axis=1)

    real, imag = plane(0), plane(1)
    real_high, real_low = halves(real)
    imag_high, imag_low = halves(imag)
    high = jnp.concatenate([real_high, imag_high], axis=0)
    low = jnp.concatenate([real_low, imag_low], axis=0)
    turned_high = jnp.concatenate([-imag_high, real_high], axis=0)
    turned_low = jnp.concatenate([-imag_low, real_low], axis=0)
    high_t, low_t = high.T, low.T
    dot = functools.partial(lax.dot_general, dimension_numbers=NN, preferred_element_type=jnp.float32)
    for which, (other_high, other_low) in enumerate([(high, low), (turned_high, turned_low)]):
        total = dot(high_t, other_high) + dot(high_t, other_low) + dot(low_t, other_high)
        out_ref[0, which] = total * scale


def correlate_chunk(got, held, start, owned, sizes, spectra):
    tm_count, chan_count, blocks, per, inputs = sizes
    channels = per // 2
    everyone = chan_count * inputs
    rows = got.shape[0] * got.shape[1] * got.shape[2]
    first = start // channels
    operands = [got.reshape(rows, LANES)]
    in_specs = [pl.BlockSpec((rows, LANES), lambda c: (0, 0))]
    aliases = {}
    if held is not None:
        operands.append(held)
        in_specs.append(pl.BlockSpec(memory_space=pl.ANY))
        aliases = {1: 0}
    return pl.pallas_call(
        functools.partial(correlate_kernel, sizes, 1.0 / spectra),
        grid=(channels,),
        in_specs=in_specs,
        out_specs=pl.BlockSpec((1, 2, everyone, everyone), lambda c: (start + c, 0, 0, 0)),
        out_shape=jax.ShapeDtypeStruct((owned, 2, everyone, everyone), jnp.float32),
        input_output_aliases=aliases,
        compiler_params=params(40),
        cost_estimate=pl.CostEstimate(
            flops=6 * channels * 2 * everyone * everyone * 2 * spectra,
            bytes_accessed=channels * 8 * everyone * everyone + 4 * rows * LANES,
            transcendentals=0,
        ),
        name="correlate_chunk",
    )(*operands)


def phases(frame, owners, owned, chunk):
    samples = np.arange(frame)
    outer = 2.0 * np.pi * ((np.arange(owners)[:, None] * owned * samples) % frame) / frame
    inner = 2.0 * np.pi * ((np.arange(owned)[:, None] * samples) % frame) / frame
    scale = 1.0 / np.sqrt(float(frame))
    cosine, sine = np.cos(inner) * scale, np.sin(inner) * scale
    outer = np.stack([np.cos(outer), np.sin(outer)]).astype(np.float32)
    tables = []
    for start in range(0, owned, chunk):
        here = slice(start, start + chunk)
        first = np.concatenate([cosine[here], -sine[here]]).astype(np.float32)
        second = np.concatenate([-sine[here], -cosine[here]]).astype(np.float32)
        tables.append((start, first, second))
    return outer, tables


def body(voltages, fir_taps):
    inputs, samples = voltages.shape
    taps, frame = fir_taps.shape
    spec_dev = samples // frame
    tm_count, chan_count = lax.axis_size("tm"), lax.axis_size("chan")
    owners = tm_count * chan_count
    owned = frame // 2 // owners
    groups = LANES // inputs
    blocks = spec_dev // groups
    chunk = max(4, owned // 4)
    halo = passed_along(voltages[:, samples - (taps - 1) * frame :], "tm", 1)
    high, low = filtered_parts(voltages, halo, fir_taps, blocks, groups)
    outer, tables = phases(frame, owners, owned, chunk)
    sizes = (tm_count, chan_count, blocks, 2 * chunk, inputs)
    moved = []
    for start, first, second in tables:
        made = dft_chunk(outer, first, second, high, low, owners, blocks)
        moved.append((start, lax.all_to_all(made, AXES, split_axis=0, concat_axis=0, tiled=True)))
    out = None
    for start, got in moved:
        out = correlate_chunk(got, out, start, owned, sizes, tm_count * spec_dev)
    return out


def solution(mesh):
    placed = (P("chan", "tm"), P())
    return jax.shard_map(
        body,
        mesh=mesh,
        in_specs=placed,
        out_specs=P(("tm", "chan"), None, None, None),
        check_vma=False,
    )
```

```python
import functools
import math

import jax
import jax.numpy as jnp
import numpy as np
from jax import lax
from jax.experimental import pallas as pl
from jax.experimental.pallas import tpu as pltpu
from jax.sharding import PartitionSpec as P

LANES = 128
AXES = ("tm", "chan")
WIDE = 2
LATE = 4
NT = (((1,), (1,)), ((), ()))
NN = (((1,), (0,)), ((), ()))


def params(mib):
    return pltpu.CompilerParams(vmem_limit_bytes=mib << 20)


def halves(value):
    high = value.astype(jnp.bfloat16)
    low = (value - high.astype(jnp.float32)).astype(jnp.bfloat16)
    return high, low


def passed_along(value, axis, steps):
    count = lax.axis_size(axis)
    first, last = (max(0, -steps), min(count, count - steps))
    return lax.ppermute(value, axis, [(source, source + steps) for source in range(first, last)])


def filter_kernel(blocks, groups, taps, volt_ref, halo_ref, fir_ref, high_ref, low_ref):
    frame = fir_ref.shape[1]
    edge = taps - 1

    def put(spec, terms):
        total = terms[0] * fir_ref[0:1, :]
        for tap in range(1, taps):
            total = total + terms[tap] * fir_ref[tap : tap + 1, :]
        high, low = halves(total)
        at = (lax.rem(spec, blocks), lax.div(spec, blocks))
        high_ref[at] = high
        low_ref[at] = low

    def old(spec):
        if spec < 0:
            return halo_ref[:, (spec + edge) * frame : (spec + edge + 1) * frame]
        return volt_ref[:, spec * frame : (spec + 1) * frame]

    for spec in range(edge):
        put(spec, [old(spec - tap) for tap in range(taps)])

    def step(spec, carry):
        put(
            spec,
            [
                volt_ref[:, pl.ds(pl.multiple_of((spec - tap) * frame, frame), frame)]
                for tap in range(taps)
            ],
        )
        return carry

    lax.fori_loop(edge, blocks * groups, step, 0)


def filtered_parts(voltages, halo, fir_taps, blocks, groups):
    inputs, samples = voltages.shape
    taps, frame = fir_taps.shape
    rows = 16
    shape = jax.ShapeDtypeStruct((blocks, groups, inputs, frame), jnp.bfloat16)
    out_spec = pl.BlockSpec((blocks, groups, rows, frame), lambda g: (0, 0, g, 0))
    high, low = pl.pallas_call(
        functools.partial(filter_kernel, blocks, groups, taps),
        grid=(inputs // rows,),
        in_specs=[
            pl.BlockSpec((rows, samples), lambda g: (g, 0)),
            pl.BlockSpec((rows, halo.shape[1]), lambda g: (g, 0)),
            pl.BlockSpec((taps, frame), lambda g: (0, 0)),
        ],
        out_specs=[out_spec, out_spec],
        out_shape=[shape, shape],
        compiler_params=params(40),
        cost_estimate=pl.CostEstimate(
            flops=8 * inputs * samples, bytes_accessed=8 * inputs * samples, transcendentals=0
        ),
        name="polyphase_filter",
    )(voltages, halo, fir_taps)
    rows_all = blocks * groups * inputs
    return high.reshape(rows_all, frame), low.reshape(rows_all, frame)


def fill_table(owners, per, outer_ref, first_ref, second_ref, high_ref, low_ref):
    many = 16 // math.gcd(per, 16)

    def rows(step, carry):
        parts = []
        for extra in range(many):
            owner = step * many + extra
            cosine = outer_ref[0, pl.ds(owner, 1), :]
            sine = outer_ref[1, pl.ds(owner, 1), :]
            parts.append(first_ref[...] * cosine + second_ref[...] * sine)
        value = parts[0] if many == 1 else jnp.concatenate(parts, axis=0)
        high, low = halves(value)
        at = pl.ds(pl.multiple_of(step * many * per, many * per), many * per)
        high_ref[at, :] = high
        low_ref[at, :] = low
        return carry

    lax.fori_loop(0, owners // many, rows, 0)


def transform(owners, per, table_high, table_low, high, low, out_ref):
    dot = functools.partial(lax.dot_general, dimension_numbers=NT, preferred_element_type=jnp.float32)
    total = dot(table_high[...], high) + dot(table_high[...], low) + dot(table_low[...], high)
    for block in range(WIDE):
        part = total[:, block * LANES : (block + 1) * LANES]
        out_ref[:, block * per : (block + 1) * per, :] = part.reshape(owners, per, LANES)


def dft_kernel(owners, per, outer_ref, first_ref, second_ref, high_ref, low_ref, *rest):
    out_ref, th_ref, tl_ref = rest[-3:]

    @pl.when(pl.program_id(0) == 0)
    def _():
        fill_table(owners, per, outer_ref, first_ref, second_ref, th_ref, tl_ref)

    transform(owners, per, th_ref, tl_ref, high_ref[...], low_ref[...], out_ref)


def dft_chunk(outer, first, second, high, low, blocks, held, base, total_rows, token=None):
    per, frame = first.shape
    owners = outer.shape[1]
    rows = WIDE * LANES
    skip = base // (WIDE * per)
    const = lambda b: (0, 0)
    operands = [outer, first, second, high, low]
    in_specs = [
        pl.BlockSpec((2, owners, frame), lambda b: (0, 0, 0)),
        pl.BlockSpec((per, frame), const),
        pl.BlockSpec((per, frame), const),
        pl.BlockSpec((rows, frame), lambda b: (b, 0)),
        pl.BlockSpec((rows, frame), lambda b: (b, 0)),
    ]
    aliases = {}
    if held is not None:
        operands.append(held)
        in_specs.append(pl.BlockSpec(memory_space=pl.ANY))
        aliases = {5: 0}
    if token is not None:
        operands.append(token)
        in_specs.append(pl.BlockSpec(memory_space=pl.ANY))
    return pl.pallas_call(
        functools.partial(dft_kernel, owners, per),
        grid=(blocks // WIDE,),
        in_specs=in_specs,
        out_specs=pl.BlockSpec((owners, WIDE * per, LANES), lambda b: (0, skip + b, 0)),
        out_shape=jax.ShapeDtypeStruct((owners, total_rows, LANES), jnp.float32),
        input_output_aliases=aliases,
        scratch_shapes=[
            pltpu.VMEM((owners * per, frame), jnp.bfloat16),
            pltpu.VMEM((owners * per, frame), jnp.bfloat16),
        ],
        compiler_params=params(48),
        cost_estimate=pl.CostEstimate(
            flops=6 * owners * per * frame * blocks * LANES,
            bytes_accessed=4 * blocks * LANES * frame + 4 * owners * blocks * per * LANES,
            transcendentals=0,
        ),
        name="dft_chunk",
    )(*operands)


def first_kernel(owners, per, taps, groups, *refs):
    now, before = refs[:groups], refs[groups : 2 * groups]
    fir_ref, outer_ref, first_ref, second_ref, out_ref = refs[2 * groups : 2 * groups + 5]
    th_ref, tl_ref, past_ref, high_ref, low_ref = refs[2 * groups + 5 :]
    inputs = now[0].shape[0]
    frame = fir_ref.shape[1]
    edge = taps - 1

    @pl.when(pl.program_id(0) == 0)
    def _():
        fill_table(owners, per, outer_ref, first_ref, second_ref, th_ref, tl_ref)
        for group in range(groups):
            past_ref[group] = before[group][:, (LATE - edge) * frame :]

    rows = 16

    def step(index, carry):
        at = pl.ds(pl.multiple_of(index * rows, rows), rows)
        for group in range(groups):

            def sample(spec):
                if spec < 0:
                    return past_ref[group, at, (spec + edge) * frame : (spec + edge + 1) * frame]
                return now[group][at, spec * frame : (spec + 1) * frame]

            for spec in range(WIDE):
                total = sample(spec) * fir_ref[0:1, :]
                for tap in range(1, taps):
                    total = total + sample(spec - tap) * fir_ref[tap : tap + 1, :]
                high, low = halves(total)
                place = pl.ds(pl.multiple_of(spec * LANES + group * inputs + index * rows, rows), rows)
                high_ref[place, :] = high
                low_ref[place, :] = low
            kept = [sample(WIDE - edge + k) for k in range(edge)]
            for k in range(edge):
                past_ref[group, at, k * frame : (k + 1) * frame] = kept[k]
        return carry

    lax.fori_loop(0, inputs // rows, step, 0)
    transform(owners, per, th_ref, tl_ref, high_ref[...], low_ref[...], out_ref)


def first_chunk(outer, first, second, voltages, fir_taps, blocks, groups):
    per, frame = first.shape
    owners = outer.shape[1]
    inputs, samples = voltages.shape
    taps = fir_taps.shape[0]
    kept = blocks - LATE
    const = lambda b: (0, 0)

    def now_map(group):
        return lambda b: (0, (group * blocks + LATE) // WIDE + b)

    def before_map(group):
        return lambda b: (0, group * blocks // LATE)

    return pl.pallas_call(
        functools.partial(first_kernel, owners, per, taps, groups),
        grid=(kept // WIDE,),
        in_specs=[pl.BlockSpec((inputs, WIDE * frame), now_map(g)) for g in range(groups)]
        + [pl.BlockSpec((inputs, LATE * frame), before_map(g)) for g in range(groups)]
        + [
            pl.BlockSpec((taps, frame), const),
            pl.BlockSpec((2, owners, frame), lambda b: (0, 0, 0)),
            pl.BlockSpec((per, frame), const),
            pl.BlockSpec((per, frame), const),
        ],
        out_specs=pl.BlockSpec((owners, WIDE * per, LANES), lambda b: (0, b, 0)),
        out_shape=jax.ShapeDtypeStruct((owners, kept * per, LANES), jnp.float32),
        scratch_shapes=[
            pltpu.VMEM((owners * per, frame), jnp.bfloat16),
            pltpu.VMEM((owners * per, frame), jnp.bfloat16),
            pltpu.VMEM((groups, inputs, (taps - 1) * frame), jnp.float32),
            pltpu.VMEM((WIDE * LANES, frame), jnp.bfloat16),
            pltpu.VMEM((WIDE * LANES, frame), jnp.bfloat16),
        ],
        compiler_params=params(48),
        cost_estimate=pl.CostEstimate(
            flops=6 * owners * per * frame * kept * LANES,
            bytes_accessed=4 * inputs * samples,
            transcendentals=0,
        ),
        name="first_chunk",
    )(*([voltages] * (2 * groups)), fir_taps, outer, first, second)


def correlate_kernel(sizes, scale, places, *refs):
    tm_count, chan_count, blocks, per, inputs = sizes
    out_ref, token_ref, got_ref, sems = refs[-4:]
    channel = pl.program_id(0)
    groups = LANES // inputs
    channels = per // 2

    @pl.when(channel == 0)
    def _():
        copies = []
        for index, (base, rows, into) in enumerate(places):
            source = refs[index].at[:, pl.ds(base, rows), :]
            target = got_ref.at[:, pl.ds(into, rows), :]
            copies.append(pltpu.make_async_copy(source, target, sems.at[index]))
            copies[-1].start()
        for copy in copies:
            copy.wait()
        token_ref[...] = jnp.zeros_like(token_ref)

    lane_group = lax.broadcasted_iota(jnp.int32, (blocks, LANES), 1) // inputs

    def piece(time, chan, part):
        rows = pl.ds(part * channels + channel, blocks, stride=per)
        return got_ref[time * chan_count + chan, rows, :]

    def tile(time, part, column):
        held = [piece(time, column * groups + place, part) for place in range(groups)]
        made = []
        for group in range(groups):
            total = None
            for place in range(groups):
                turn = (place - group) * inputs % LANES
                value = pltpu.roll(held[place], turn, 1) if turn else held[place]
                total = value if total is None else jnp.where(lane_group == place, value, total)
            made.append(total)
        return jnp.concatenate(made, axis=0)

    def plane(part):
        columns = []
        for column in range(chan_count // groups):
            columns.append(
                jnp.concatenate([tile(time, part, column) for time in range(tm_count)], axis=0)
            )
        return jnp.concatenate(columns, axis=1)

    real, imag = plane(0), plane(1)
    real_high, real_low = halves(real)
    imag_high, imag_low = halves(imag)
    high = jnp.concatenate([real_high, imag_high], axis=0)
    low = jnp.concatenate([real_low, imag_low], axis=0)
    turned_high = jnp.concatenate([-imag_high, real_high], axis=0)
    turned_low = jnp.concatenate([-imag_low, real_low], axis=0)
    high_t, low_t = high.T, low.T
    dot = functools.partial(lax.dot_general, dimension_numbers=NN, preferred_element_type=jnp.float32)
    for which, (other_high, other_low) in enumerate([(high, low), (turned_high, turned_low)]):
        total = dot(high_t, other_high) + dot(high_t, other_low) + dot(low_t, other_high)
        out_ref[0, which] = total * scale


def correlate_chunk(pieces, held, start, owned, sizes, spectra):
    tm_count, chan_count, blocks, per, inputs = sizes
    channels = per // 2
    everyone = chan_count * inputs
    owners = tm_count * chan_count
    operands = [piece[0] for piece in pieces]
    places = [piece[1:] for piece in pieces]
    aliases = {}
    if held is not None:
        aliases = {len(operands): 0}
        operands.append(held)
    return pl.pallas_call(
        functools.partial(correlate_kernel, sizes, 1.0 / spectra, places),
        grid=(channels,),
        in_specs=[pl.BlockSpec(memory_space=pl.ANY)] * len(operands),
        out_specs=[
            pl.BlockSpec((1, 2, everyone, everyone), lambda c: (start + c, 0, 0, 0)),
            pl.BlockSpec((8, LANES), lambda c: (0, 0)),
        ],
        out_shape=[
            jax.ShapeDtypeStruct((owned, 2, everyone, everyone), jnp.float32),
            jax.ShapeDtypeStruct((8, LANES), jnp.float32),
        ],
        input_output_aliases=aliases,
        scratch_shapes=[
            pltpu.VMEM((owners, blocks * per, LANES), jnp.float32),
            pltpu.SemaphoreType.DMA((len(pieces),)),
        ],
        compiler_params=params(40),
        cost_estimate=pl.CostEstimate(
            flops=6 * channels * 2 * everyone * everyone * 2 * spectra,
            bytes_accessed=channels * 8 * everyone * everyone + 4 * owners * blocks * per * LANES,
            transcendentals=0,
        ),
        name="correlate_chunk",
    )(*operands)


def chunk_sizes(owned):
    if owned % 32 == 0:
        return [owned // 8, owned // 4, owned // 2, owned // 8]
    return [4] * (owned // 4)


def phases(frame, owners, owned, sizes):
    samples = np.arange(frame)
    outer = 2.0 * np.pi * ((np.arange(owners)[:, None] * owned * samples) % frame) / frame
    inner = 2.0 * np.pi * ((np.arange(owned)[:, None] * samples) % frame) / frame
    scale = 1.0 / np.sqrt(float(frame))
    cosine, sine = np.cos(inner) * scale, np.sin(inner) * scale
    outer = np.stack([np.cos(outer), np.sin(outer)]).astype(np.float32)
    tables = []
    start = 0
    for size in sizes:
        here = slice(start, start + size)
        first = np.concatenate([cosine[here], -sine[here]]).astype(np.float32)
        second = np.concatenate([-sine[here], -cosine[here]]).astype(np.float32)
        tables.append((start, first, second))
        start += size
    return outer, tables


def body(voltages, fir_taps):
    inputs, samples = voltages.shape
    taps, frame = fir_taps.shape
    spec_dev = samples // frame
    tm_count, chan_count = lax.axis_size("tm"), lax.axis_size("chan")
    owners = tm_count * chan_count
    owned = frame // 2 // owners
    groups = LANES // inputs
    blocks = spec_dev // groups
    chunks = chunk_sizes(owned)
    outer, tables = phases(frame, owners, owned, chunks)
    split = blocks >= 2 * LATE and len(chunks) > 1

    def exchange(value):
        return lax.all_to_all(value, AXES, split_axis=0, concat_axis=0, tiled=True)

    halo = passed_along(voltages[:, samples - (taps - 1) * frame :], "tm", 1)
    if split:
        ahead = first_chunk(outer, *tables[0][1:], voltages, fir_taps, blocks, groups)
        ahead, halo = lax.optimization_barrier((ahead, halo))
    high, low = filtered_parts(voltages, halo, fir_taps, blocks, groups)

    pieces = [[] for _ in chunks]
    out, token, correlated = None, None, 0

    def correlate(index):
        nonlocal out, token
        sizes = (tm_count, chan_count, blocks, 2 * chunks[index], inputs)
        out, token = correlate_chunk(
            pieces[index], out, tables[index][0], owned, sizes, tm_count * spec_dev
        )

    for index, (start, first, second) in enumerate(tables):
        per = 2 * chunks[index]
        rows = blocks * per
        if index == 0 and split:
            got = exchange(ahead)
            pieces[0].append((got, 0, (blocks - LATE) * per, LATE * per))
            continue
        while correlated <= index - 2 and (index > 2 or not split):
            correlate(correlated)
            correlated += 1
        if index == 1 and split:
            more = LATE * 2 * chunks[0]
            made = dft_chunk(outer, *tables[0][1:], high, low, LATE, None, rows, rows + more)
            made = dft_chunk(outer, first, second, high, low, blocks, made, 0, rows + more)
        else:
            more = 0
            made = dft_chunk(outer, first, second, high, low, blocks, None, 0, rows, token)
        got = exchange(made)
        if more:
            pieces[0].append((got, rows, more, 0))
        pieces[index].append((got, 0, rows, 0))
    while correlated < len(chunks):
        correlate(correlated)
        correlated += 1
    return out


def solution(mesh):
    placed = (P("chan", "tm"), P())
    return jax.shard_map(
        body,
        mesh=mesh,
        in_specs=placed,
        out_specs=P(("tm", "chan"), None, None, None),
        check_vma=False,
    )
```

```python
import functools
import math

import jax
import jax.numpy as jnp
import numpy as np
from jax import lax
from jax.experimental import pallas as pl
from jax.experimental.pallas import tpu as pltpu
from jax.sharding import PartitionSpec as P

LANES = 128
AXES = ("tm", "chan")
PAIR = 2
WIDE = 2
LATE = 6
NT = (((1,), (1,)), ((), ()))
NN = (((1,), (0,)), ((), ()))


def params(mib):
    return pltpu.CompilerParams(vmem_limit_bytes=mib << 20)


def halves(value):
    high = value.astype(jnp.bfloat16)
    low = (value - high.astype(jnp.float32)).astype(jnp.bfloat16)
    return high, low


def passed_along(value, axis, steps):
    count = lax.axis_size(axis)
    first, last = (max(0, -steps), min(count, count - steps))
    return lax.ppermute(value, axis, [(source, source + steps) for source in range(first, last)])


def weighted(frames, weights):
    total = frames[0] * weights[0]
    for frame, weight in zip(frames[1:], weights[1:]):
        total = total + frame * weight
    return total


def folded(left, right):
    return halves(left + right) + halves(left - right)


def filter_kernel(blocks, groups, taps, volt_ref, halo_ref, fir_ref, *out_refs):
    rows = volt_ref.shape[0]
    frame = fir_ref.shape[1]
    edge = taps - 1
    width = 2 * LANES

    def columns(column, carry):
        begins = [pl.multiple_of(column * width, width), pl.multiple_of(column * width + frame // 2, width)]
        here = pl.ds(begins[0], width)
        weights = [
            [jnp.broadcast_to(fir_ref[tap : tap + 1, pl.ds(begin, width)], (rows, width)) for tap in range(taps)]
            for begin in begins
        ]

        def step(spec, past):
            now = [volt_ref[:, pl.ds(pl.multiple_of(spec * frame + begin, width), width)] for begin in begins]
            sides = [weighted((now[k],) + past[k], weights[k]) for k in range(2)]
            block, group = lax.rem(spec, blocks), lax.div(spec, blocks)
            for ref, value in zip(out_refs, folded(*sides)):
                ref[block, group, :, here] = value
            return tuple((now[k],) + past[k][:-1] for k in range(2))

        past = tuple(
            tuple(
                halo_ref[:, pl.ds(pl.multiple_of((edge - 1 - k) * frame + begin, width), width)]
                for k in range(edge)
            )
            for begin in begins
        )
        lax.fori_loop(0, blocks * groups, step, past, unroll=4)
        return carry

    lax.fori_loop(0, frame // 2 // width, columns, 0)


def filtered_parts(voltages, halo, fir_taps, blocks, groups):
    inputs, samples = voltages.shape
    taps, frame = fir_taps.shape
    rows = 16
    shape = jax.ShapeDtypeStruct((blocks, groups, inputs, frame // 2), jnp.bfloat16)
    out_spec = pl.BlockSpec((blocks, groups, rows, frame // 2), lambda g: (0, 0, g, 0))
    made = pl.pallas_call(
        functools.partial(filter_kernel, blocks, groups, taps),
        grid=(inputs // rows,),
        in_specs=[
            pl.BlockSpec((rows, samples), lambda g: (g, 0)),
            pl.BlockSpec((rows, halo.shape[1]), lambda g: (g, 0)),
            pl.BlockSpec((taps, frame), lambda g: (0, 0)),
        ],
        out_specs=[out_spec] * 4,
        out_shape=[shape] * 4,
        compiler_params=params(48),
        cost_estimate=pl.CostEstimate(
            flops=8 * inputs * samples, bytes_accessed=8 * inputs * samples, transcendentals=0
        ),
        name="polyphase_filter",
    )(voltages, halo, fir_taps)
    made = [part.reshape(blocks * groups * inputs, frame // 2) for part in made]
    return made[:2], made[2:]


def fill_table(owners, per, outer_ref, first_ref, second_ref, high_ref, low_ref):
    many = 16 // math.gcd(per, 16)

    def rows(step, carry):
        parts = []
        for extra in range(many):
            owner = step * many + extra
            cosine = outer_ref[0, pl.ds(owner, 1), :]
            sine = outer_ref[1, pl.ds(owner, 1), :]
            parts.append(first_ref[...] * cosine + second_ref[...] * sine)
        value = parts[0] if many == 1 else jnp.concatenate(parts, axis=0)
        high, low = halves(value)
        at = pl.ds(pl.multiple_of(step * many * per, many * per), many * per)
        high_ref[at, :] = high
        low_ref[at, :] = low
        return carry

    lax.fori_loop(0, owners // many, rows, 0)


def transform(owners, per, table_high, table_low, high, low, out_ref):
    dot = functools.partial(lax.dot_general, dimension_numbers=NT, preferred_element_type=jnp.float32)
    total = dot(table_high[...], high) + dot(table_high[...], low) + dot(table_low[...], high)
    for block in range(WIDE):
        part = total[:, block * LANES : (block + 1) * LANES]
        out_ref[:, block * per : (block + 1) * per, :] = part.reshape(owners, per, LANES)


def dft_kernel(owners, per, outer_ref, first_ref, second_ref, high_ref, low_ref, *rest):
    out_ref, th_ref, tl_ref = rest[-3:]

    @pl.when(pl.program_id(0) == 0)
    def _():
        fill_table(owners, per, outer_ref, first_ref, second_ref, th_ref, tl_ref)

    transform(owners, per, th_ref, tl_ref, high_ref[...], low_ref[...], out_ref)


def dft_chunk(outer, first, second, high, low, blocks, held, base, total_rows, token=None):
    per, frame = first.shape
    owners = outer.shape[1]
    rows = WIDE * LANES
    assert base % (WIDE * per) == 0
    skip = base // (WIDE * per)
    const = lambda b: (0, 0)
    operands = [outer, first, second, high, low]
    in_specs = [
        pl.BlockSpec((2, owners, frame), lambda b: (0, 0, 0)),
        pl.BlockSpec((per, frame), const),
        pl.BlockSpec((per, frame), const),
        pl.BlockSpec((rows, frame), lambda b: (b, 0)),
        pl.BlockSpec((rows, frame), lambda b: (b, 0)),
    ]
    aliases = {}
    if held is not None:
        operands.append(held)
        in_specs.append(pl.BlockSpec(memory_space=pl.ANY))
        aliases = {5: 0}
    if token is not None:
        operands.append(token)
        in_specs.append(pl.BlockSpec(memory_space=pl.ANY))
    return pl.pallas_call(
        functools.partial(dft_kernel, owners, per),
        grid=(blocks // WIDE,),
        in_specs=in_specs,
        out_specs=pl.BlockSpec((owners, WIDE * per, LANES), lambda b: (0, skip + b, 0)),
        out_shape=jax.ShapeDtypeStruct((owners, total_rows, LANES), jnp.float32),
        input_output_aliases=aliases,
        scratch_shapes=[
            pltpu.VMEM((owners * per, frame), jnp.bfloat16),
            pltpu.VMEM((owners * per, frame), jnp.bfloat16),
        ],
        compiler_params=params(60),
        cost_estimate=pl.CostEstimate(
            flops=6 * owners * per * frame * blocks * LANES,
            bytes_accessed=4 * blocks * LANES * frame + 4 * owners * blocks * per * LANES,
            transcendentals=0,
        ),
        name="dft_chunk",
    )(*operands)


def first_kernel(owners, per, taps, groups, *refs):
    now = refs[:groups]
    fir_ref, outer_ref, first_ref, second_ref, out_ref = refs[groups : groups + 5]
    th_ref, tl_ref, past_ref, high_ref, low_ref = refs[groups + 5 :]
    inputs = now[0].shape[0]
    frame = fir_ref.shape[1]
    edge = taps - 1
    pair = pl.program_id(0)
    ahead = pl.cdiv(edge, WIDE)

    @pl.when(pair == 0)
    def _():
        fill_table(owners, per, outer_ref, first_ref, second_ref, th_ref, tl_ref)

    @pl.when(pair < ahead)
    def _():
        @pl.when(pair > 0)
        def _():
            for k in range(edge - WIDE):
                past_ref[k] = past_ref[k + WIDE]

        for group in range(groups):
            for k in range(WIDE):
                past_ref[edge - WIDE + k, group] = now[group][:, k * frame : (k + 1) * frame]

    @pl.when(pair >= ahead)
    def _():
        rows = 16
        width = 2 * LANES

        def columns(column, carry):
            begins = [
                pl.multiple_of(column * width, width),
                pl.multiple_of(column * width + frame // 2, width),
            ]
            weights = [
                [
                    jnp.broadcast_to(fir_ref[tap : tap + 1, pl.ds(begin, width)], (rows, width))
                    for tap in range(taps)
                ]
                for begin in begins
            ]
            for group in range(groups):
                for start in range(0, inputs, rows):
                    at = pl.ds(start, rows)
                    sums = [None] * WIDE
                    for begin, weight in zip(begins, weights):
                        here = pl.ds(begin, width)
                        frames = [past_ref[k, group, at, here] for k in range(edge)]
                        for spec in range(WIDE):
                            frames.append(
                                now[group][at, pl.ds(pl.multiple_of(spec * frame + begin, width), width)]
                            )
                        for spec in range(WIDE):
                            total = weighted([frames[edge + spec - tap] for tap in range(taps)], weight)
                            sums[spec] = total if sums[spec] is None else sums[spec] + total
                        for k in range(edge):
                            past_ref[k, group, at, here] = frames[WIDE + k]
                    for spec in range(WIDE):
                        high, low = halves(sums[spec])
                        place = pl.ds(spec * LANES + group * inputs + start, rows)
                        high_ref[place, pl.ds(begins[0], width)] = high
                        low_ref[place, pl.ds(begins[0], width)] = low
            return carry

        lax.fori_loop(0, frame // 2 // width, columns, 0)
        transform(owners, per, th_ref, tl_ref, high_ref[...], low_ref[...], out_ref)


def first_chunk(outer, first, second, voltages, fir_taps, blocks, groups):
    per, half = first.shape
    owners = outer.shape[1]
    inputs, samples = voltages.shape
    taps, frame = fir_taps.shape
    kept = blocks - LATE
    const = lambda b: (0, 0)

    ahead = pl.cdiv(taps - 1, WIDE)

    def now_map(group):
        return lambda b: (0, (group * blocks + LATE) // WIDE - ahead + b)

    return pl.pallas_call(
        functools.partial(first_kernel, owners, per, taps, groups),
        grid=(kept // WIDE + ahead,),
        in_specs=[pl.BlockSpec((inputs, WIDE * frame), now_map(g)) for g in range(groups)]
        + [
            pl.BlockSpec((taps, frame), const),
            pl.BlockSpec((2, owners, half), lambda b: (0, 0, 0)),
            pl.BlockSpec((per, half), const),
            pl.BlockSpec((per, half), const),
        ],
        out_specs=pl.BlockSpec((owners, WIDE * per, LANES), lambda b: (0, jnp.maximum(b - ahead, 0), 0)),
        out_shape=jax.ShapeDtypeStruct((owners, kept * per, LANES), jnp.float32),
        scratch_shapes=[
            pltpu.VMEM((owners * per, half), jnp.bfloat16),
            pltpu.VMEM((owners * per, half), jnp.bfloat16),
            pltpu.VMEM((taps - 1, groups, inputs, frame), jnp.float32),
            pltpu.VMEM((WIDE * LANES, half), jnp.bfloat16),
            pltpu.VMEM((WIDE * LANES, half), jnp.bfloat16),
        ],
        compiler_params=params(60),
        cost_estimate=pl.CostEstimate(
            flops=6 * owners * per * half * kept * LANES,
            bytes_accessed=4 * inputs * samples,
            transcendentals=0,
        ),
        name="first_chunk",
    )(*([voltages] * groups), fir_taps, outer, first, second)


def correlate_kernel(sizes, scale, places, *refs):
    tm_count, chan_count, blocks, per, inputs = sizes
    out_ref, token_ref, got_ref, sems = refs[-4:]
    groups = LANES // inputs
    channels = per // 2

    @pl.when(pl.program_id(0) == 0)
    def _():
        copies = []
        for index, (base, rows, into) in enumerate(places):
            source = refs[index].at[:, pl.ds(base, rows), :]
            target = got_ref.at[:, pl.ds(into, rows), :]
            copies.append(pltpu.make_async_copy(source, target, sems.at[index]))
            copies[-1].start()
        for copy in copies:
            copy.wait()
        token_ref[...] = jnp.zeros_like(token_ref)

    lane_group = lax.broadcasted_iota(jnp.int32, (blocks, LANES), 1) // inputs

    def piece(channel, time, chan, part):
        rows = pl.ds(part * channels + channel, blocks, stride=per)
        return got_ref[time * chan_count + chan, rows, :]

    def tile(channel, time, part, column):
        held = [piece(channel, time, column * groups + place, part) for place in range(groups)]
        made = []
        for group in range(groups):
            total = None
            for place in range(groups):
                turn = (place - group) * inputs % LANES
                value = pltpu.roll(held[place], turn, 1) if turn else held[place]
                total = value if total is None else jnp.where(lane_group == place, value, total)
            made.append(total)
        return jnp.concatenate(made, axis=0)

    def plane(channel, part):
        columns = []
        for column in range(chan_count // groups):
            columns.append(
                jnp.concatenate([tile(channel, time, part, column) for time in range(tm_count)], axis=0)
            )
        return jnp.concatenate(columns, axis=1)

    dot = functools.partial(lax.dot_general, dimension_numbers=NN, preferred_element_type=jnp.float32)
    for sub in range(PAIR):
        channel = pl.program_id(0) * PAIR + sub
        real, imag = plane(channel, 0), plane(channel, 1)
        real_high, real_low = halves(real)
        imag_high, imag_low = halves(imag)
        high = jnp.concatenate([real_high, imag_high], axis=0)
        low = jnp.concatenate([real_low, imag_low], axis=0)
        turned_high = jnp.concatenate([-imag_high, real_high], axis=0)
        turned_low = jnp.concatenate([-imag_low, real_low], axis=0)
        high_t, low_t = high.T, low.T
        for which, (other_high, other_low) in enumerate([(high, low), (turned_high, turned_low)]):
            total = dot(high_t, other_high) + dot(high_t, other_low) + dot(low_t, other_high)
            out_ref[sub, 0, which] = total * scale


def correlate_chunk(pieces, held, start, owned, sizes, spectra):
    tm_count, chan_count, blocks, per, inputs = sizes
    channels = per // 2
    everyone = chan_count * inputs
    owners = tm_count * chan_count
    operands = [piece[0] for piece in pieces]
    places = [piece[1:] for piece in pieces]
    aliases = {}
    if held is not None:
        aliases = {len(operands): 0}
        operands.append(held)
    return pl.pallas_call(
        functools.partial(correlate_kernel, sizes, 1.0 / spectra, places),
        grid=(channels // PAIR,),
        in_specs=[pl.BlockSpec(memory_space=pl.ANY)] * len(operands),
        out_specs=[
            pl.BlockSpec((PAIR, 1, 2, everyone, everyone), lambda c: (start // 2 // PAIR + c, start % 2, 0, 0, 0)),
            pl.BlockSpec((8, LANES), lambda c: (0, 0)),
        ],
        out_shape=[
            jax.ShapeDtypeStruct((owned // 2, 2, 2, everyone, everyone), jnp.float32),
            jax.ShapeDtypeStruct((8, LANES), jnp.float32),
        ],
        input_output_aliases=aliases,
        scratch_shapes=[
            pltpu.VMEM((owners, blocks * per, LANES), jnp.float32),
            pltpu.SemaphoreType.DMA((len(pieces),)),
        ],
        compiler_params=params(60),
        cost_estimate=pl.CostEstimate(
            flops=6 * channels * 2 * everyone * everyone * 2 * spectra,
            bytes_accessed=channels * 8 * everyone * everyone + 4 * owners * blocks * per * LANES,
            transcendentals=0,
        ),
        name="correlate_chunk",
    )(*operands)


def chunk_plan(owned):
    unit = owned // 8
    if owned % 32 == 0:
        return [[(0, 2 * unit)], [(2 * unit + 1, 3 * unit), (4 * unit, 2 * unit)], [(1, unit)]]
    return [[(parity, owned // 2)] for parity in (0, 1)]


def phases(frame, owners, owned, segments):
    samples = np.arange(frame // 2)
    outer = 2.0 * np.pi * ((np.arange(owners)[:, None] * owned * samples) % frame) / frame
    outer = np.stack([np.cos(outer), np.sin(outer)]).astype(np.float32)
    scale = 1.0 / np.sqrt(float(frame))
    tables = {}
    for start, count in segments:
        channels = start + 2 * np.arange(count)
        inner = 2.0 * np.pi * ((channels[:, None] * samples) % frame) / frame
        cosine, sine = np.cos(inner) * scale, np.sin(inner) * scale
        first = np.concatenate([cosine, -sine]).astype(np.float32)
        second = np.concatenate([-sine, -cosine]).astype(np.float32)
        tables[start, count] = (first, second)
    return outer, tables


def body(voltages, fir_taps):
    inputs, samples = voltages.shape
    taps, frame = fir_taps.shape
    spec_dev = samples // frame
    tm_count, chan_count = lax.axis_size("tm"), lax.axis_size("chan")
    owners = tm_count * chan_count
    owned = frame // 2 // owners
    groups = LANES // inputs
    blocks = spec_dev // groups
    chunks = chunk_plan(owned)
    outer, tables = phases(frame, owners, owned, sum(chunks, []))
    split = blocks > LATE and len(chunks) > 2

    def exchange(value):
        return lax.all_to_all(value, AXES, split_axis=0, concat_axis=0, tiled=True)

    halo = passed_along(voltages[:, samples - (taps - 1) * frame :], "tm", 1)
    if split:
        ahead = first_chunk(outer, *tables[chunks[0][0]], voltages, fir_taps, blocks, groups)
        ahead, halo = lax.optimization_barrier((ahead, halo))
    parts = filtered_parts(voltages, halo, fir_taps, blocks, groups)

    def transformed(segment, count, made, base, rows, token):
        return dft_chunk(
            outer, *tables[segment], *parts[segment[0] % 2], count, made, base, rows, token
        )

    pieces = {segment: [] for segment in sum(chunks, [])}
    out, token = None, None

    def correlate(segments):
        nonlocal out, token
        for segment in segments:
            start, count = segment
            sizes = (tm_count, chan_count, blocks, 2 * count, inputs)
            out, token = correlate_chunk(
                pieces[segment], out, start, owned, sizes, tm_count * spec_dev
            )

    for index, chunk in enumerate(chunks):
        if index == 0 and split:
            (segment,) = chunk
            per = 2 * segment[1]
            pieces[segment].append((exchange(ahead), 0, (blocks - LATE) * per, LATE * per))
            continue
        plan = [(segment, blocks) for segment in chunk]
        if index == 1 and split:
            plan.append((chunks[0][0], LATE))
        rows = sum(2 * segment[1] * count for segment, count in plan)
        made, base, places = None, 0, []
        for segment, count in plan:
            made = transformed(segment, count, made, base, rows, token)
            places.append((segment, base, 2 * segment[1] * count))
            base += 2 * segment[1] * count
        got = exchange(made)
        for segment, base, more in places:
            pieces[segment].append((got, base, more, 0))
    correlate(sum(chunks, []))
    return out.reshape(owned, 2, chan_count * inputs, chan_count * inputs)


def solution(mesh):
    placed = (P("chan", "tm"), P())
    return jax.shard_map(
        body,
        mesh=mesh,
        in_specs=placed,
        out_specs=P(("tm", "chan"), None, None, None),
        check_vma=False,
    )
```

```python
import functools
import math

import jax
import jax.numpy as jnp
import numpy as np
from jax import lax
from jax.experimental import pallas as pl
from jax.experimental.pallas import tpu as pltpu
from jax.sharding import PartitionSpec as P

LANES = 128
AXES = ("tm", "chan")
PAIR = 2
WIDE = 2
LATE = 6
NT = (((1,), (1,)), ((), ()))
NN = (((1,), (0,)), ((), ()))


def params(mib):
    return pltpu.CompilerParams(vmem_limit_bytes=mib << 20)


def halves(value):
    high = value.astype(jnp.bfloat16)
    low = (value - high.astype(jnp.float32)).astype(jnp.bfloat16)
    return high, low


def passed_along(value, axis, steps):
    count = lax.axis_size(axis)
    first, last = (max(0, -steps), min(count, count - steps))
    return lax.ppermute(value, axis, [(source, source + steps) for source in range(first, last)])


def weighted(frames, weights):
    total = frames[0] * weights[0]
    for frame, weight in zip(frames[1:], weights[1:]):
        total = total + frame * weight
    return total


def folded(left, right):
    return halves(left + right) + halves(left - right)


def filter_kernel(blocks, groups, taps, volt_ref, halo_ref, fir_ref, *out_refs):
    rows = volt_ref.shape[0]
    frame = fir_ref.shape[1]
    edge = taps - 1
    width = 2 * LANES

    def columns(column, carry):
        begins = [pl.multiple_of(column * width, width), pl.multiple_of(column * width + frame // 2, width)]
        here = pl.ds(begins[0], width)
        weights = [
            [jnp.broadcast_to(fir_ref[tap : tap + 1, pl.ds(begin, width)], (rows, width)) for tap in range(taps)]
            for begin in begins
        ]

        def step(spec, past):
            now = [volt_ref[:, pl.ds(pl.multiple_of(spec * frame + begin, width), width)] for begin in begins]
            sides = [weighted((now[k],) + past[k], weights[k]) for k in range(2)]
            block, group = lax.rem(spec, blocks), lax.div(spec, blocks)
            for ref, value in zip(out_refs, folded(*sides)):
                ref[block, group, :, here] = value
            return tuple((now[k],) + past[k][:-1] for k in range(2))

        past = tuple(
            tuple(
                halo_ref[:, pl.ds(pl.multiple_of((edge - 1 - k) * frame + begin, width), width)]
                for k in range(edge)
            )
            for begin in begins
        )
        lax.fori_loop(0, blocks * groups, step, past, unroll=4)
        return carry

    lax.fori_loop(0, frame // 2 // width, columns, 0)


def filtered_parts(voltages, halo, fir_taps, blocks, groups):
    inputs, samples = voltages.shape
    taps, frame = fir_taps.shape
    rows = 16
    shape = jax.ShapeDtypeStruct((blocks, groups, inputs, frame // 2), jnp.bfloat16)
    out_spec = pl.BlockSpec((blocks, groups, rows, frame // 2), lambda g: (0, 0, g, 0))
    made = pl.pallas_call(
        functools.partial(filter_kernel, blocks, groups, taps),
        grid=(inputs // rows,),
        in_specs=[
            pl.BlockSpec((rows, samples), lambda g: (g, 0)),
            pl.BlockSpec((rows, halo.shape[1]), lambda g: (g, 0)),
            pl.BlockSpec((taps, frame), lambda g: (0, 0)),
        ],
        out_specs=[out_spec] * 4,
        out_shape=[shape] * 4,
        compiler_params=params(60),
        cost_estimate=pl.CostEstimate(
            flops=8 * inputs * samples, bytes_accessed=8 * inputs * samples, transcendentals=0
        ),
        name="polyphase_filter",
    )(voltages, halo, fir_taps)
    made = [part.reshape(blocks * groups * inputs, frame // 2) for part in made]
    return made[:2], made[2:]


def fill_table(owners, per, outer_ref, first_ref, second_ref, high_ref, low_ref):
    many = 16 // math.gcd(per, 16)

    def rows(step, carry):
        parts = []
        for extra in range(many):
            owner = step * many + extra
            cosine = outer_ref[0, pl.ds(owner, 1), :]
            sine = outer_ref[1, pl.ds(owner, 1), :]
            parts.append(first_ref[...] * cosine + second_ref[...] * sine)
        value = parts[0] if many == 1 else jnp.concatenate(parts, axis=0)
        high, low = halves(value)
        at = pl.ds(pl.multiple_of(step * many * per, many * per), many * per)
        high_ref[at, :] = high
        low_ref[at, :] = low
        return carry

    lax.fori_loop(0, owners // many, rows, 0)


def transform(owners, per, table_high, table_low, high, low, out_ref):
    dot = functools.partial(lax.dot_general, dimension_numbers=NT, preferred_element_type=jnp.float32)
    total = dot(table_high[...], high) + dot(table_high[...], low) + dot(table_low[...], high)
    for block in range(high.shape[0] // LANES):
        part = total[:, block * LANES : (block + 1) * LANES]
        out_ref[:, block * per : (block + 1) * per, :] = part.reshape(owners, per, LANES)


def dft_kernel(owners, per, outer_ref, first_ref, second_ref, high_ref, low_ref, *rest):
    out_ref, th_ref, tl_ref = rest[-3:]

    @pl.when(pl.program_id(0) == 0)
    def _():
        fill_table(owners, per, outer_ref, first_ref, second_ref, th_ref, tl_ref)

    transform(owners, per, th_ref, tl_ref, high_ref[...], low_ref[...], out_ref)


def dft_chunk(outer, first, second, high, low, blocks, held, base, total_rows, token=None):
    per, frame = first.shape
    owners = outer.shape[1]
    wide = 2 * WIDE if blocks % (2 * WIDE) == 0 and base % (2 * WIDE * per) == 0 else WIDE
    rows = wide * LANES
    assert base % (wide * per) == 0
    skip = base // (wide * per)
    const = lambda b: (0, 0)
    operands = [outer, first, second, high, low]
    in_specs = [
        pl.BlockSpec((2, owners, frame), lambda b: (0, 0, 0)),
        pl.BlockSpec((per, frame), const),
        pl.BlockSpec((per, frame), const),
        pl.BlockSpec((rows, frame), lambda b: (b, 0)),
        pl.BlockSpec((rows, frame), lambda b: (b, 0)),
    ]
    aliases = {}
    if held is not None:
        operands.append(held)
        in_specs.append(pl.BlockSpec(memory_space=pl.ANY))
        aliases = {5: 0}
    if token is not None:
        operands.append(token)
        in_specs.append(pl.BlockSpec(memory_space=pl.ANY))
    return pl.pallas_call(
        functools.partial(dft_kernel, owners, per),
        grid=(blocks // wide,),
        in_specs=in_specs,
        out_specs=pl.BlockSpec((owners, wide * per, LANES), lambda b: (0, skip + b, 0)),
        out_shape=jax.ShapeDtypeStruct((owners, total_rows, LANES), jnp.float32),
        input_output_aliases=aliases,
        scratch_shapes=[
            pltpu.VMEM((owners * per, frame), jnp.bfloat16),
            pltpu.VMEM((owners * per, frame), jnp.bfloat16),
        ],
        compiler_params=params(60),
        cost_estimate=pl.CostEstimate(
            flops=6 * owners * per * frame * blocks * LANES,
            bytes_accessed=4 * blocks * LANES * frame + 4 * owners * blocks * per * LANES,
            transcendentals=0,
        ),
        name="dft_chunk",
    )(*operands)


def first_kernel(owners, per, taps, groups, *refs):
    now = refs[:groups]
    fir_ref, outer_ref, first_ref, second_ref, out_ref = refs[groups : groups + 5]
    th_ref, tl_ref, past_ref, high_ref, low_ref = refs[groups + 5 :]
    inputs = now[0].shape[0]
    frame = fir_ref.shape[1]
    edge = taps - 1
    pair = pl.program_id(0)
    ahead = pl.cdiv(edge, WIDE)

    @pl.when(pair == 0)
    def _():
        fill_table(owners, per, outer_ref, first_ref, second_ref, th_ref, tl_ref)

    @pl.when(pair < ahead)
    def _():
        @pl.when(pair > 0)
        def _():
            for k in range(edge - WIDE):
                past_ref[k] = past_ref[k + WIDE]

        for group in range(groups):
            for k in range(WIDE):
                past_ref[edge - WIDE + k, group] = now[group][:, k * frame : (k + 1) * frame]

    @pl.when(pair >= ahead)
    def _():
        rows = 16
        width = 2 * LANES

        def columns(column, carry):
            begins = [
                pl.multiple_of(column * width, width),
                pl.multiple_of(column * width + frame // 2, width),
            ]
            weights = [
                [
                    jnp.broadcast_to(fir_ref[tap : tap + 1, pl.ds(begin, width)], (rows, width))
                    for tap in range(taps)
                ]
                for begin in begins
            ]
            for group in range(groups):
                for start in range(0, inputs, rows):
                    at = pl.ds(start, rows)
                    sums = [None] * WIDE
                    for begin, weight in zip(begins, weights):
                        here = pl.ds(begin, width)
                        frames = [past_ref[k, group, at, here] for k in range(edge)]
                        for spec in range(WIDE):
                            frames.append(
                                now[group][at, pl.ds(pl.multiple_of(spec * frame + begin, width), width)]
                            )
                        for spec in range(WIDE):
                            total = weighted([frames[edge + spec - tap] for tap in range(taps)], weight)
                            sums[spec] = total if sums[spec] is None else sums[spec] + total
                        for k in range(edge):
                            past_ref[k, group, at, here] = frames[WIDE + k]
                    for spec in range(WIDE):
                        high, low = halves(sums[spec])
                        place = pl.ds(spec * LANES + group * inputs + start, rows)
                        high_ref[place, pl.ds(begins[0], width)] = high
                        low_ref[place, pl.ds(begins[0], width)] = low
            return carry

        lax.fori_loop(0, frame // 2 // width, columns, 0)
        transform(owners, per, th_ref, tl_ref, high_ref[...], low_ref[...], out_ref)


def first_chunk(outer, first, second, voltages, fir_taps, blocks, groups):
    per, half = first.shape
    owners = outer.shape[1]
    inputs, samples = voltages.shape
    taps, frame = fir_taps.shape
    kept = blocks - LATE
    const = lambda b: (0, 0)

    ahead = pl.cdiv(taps - 1, WIDE)

    def now_map(group):
        return lambda b: (0, (group * blocks + LATE) // WIDE - ahead + b)

    return pl.pallas_call(
        functools.partial(first_kernel, owners, per, taps, groups),
        grid=(kept // WIDE + ahead,),
        in_specs=[pl.BlockSpec((inputs, WIDE * frame), now_map(g)) for g in range(groups)]
        + [
            pl.BlockSpec((taps, frame), const),
            pl.BlockSpec((2, owners, half), lambda b: (0, 0, 0)),
            pl.BlockSpec((per, half), const),
            pl.BlockSpec((per, half), const),
        ],
        out_specs=pl.BlockSpec((owners, WIDE * per, LANES), lambda b: (0, jnp.maximum(b - ahead, 0), 0)),
        out_shape=jax.ShapeDtypeStruct((owners, kept * per, LANES), jnp.float32),
        scratch_shapes=[
            pltpu.VMEM((owners * per, half), jnp.bfloat16),
            pltpu.VMEM((owners * per, half), jnp.bfloat16),
            pltpu.VMEM((taps - 1, groups, inputs, frame), jnp.float32),
            pltpu.VMEM((WIDE * LANES, half), jnp.bfloat16),
            pltpu.VMEM((WIDE * LANES, half), jnp.bfloat16),
        ],
        compiler_params=params(60),
        cost_estimate=pl.CostEstimate(
            flops=6 * owners * per * half * kept * LANES,
            bytes_accessed=4 * inputs * samples,
            transcendentals=0,
        ),
        name="first_chunk",
    )(*([voltages] * groups), fir_taps, outer, first, second)


def correlate_kernel(sizes, scale, places, *refs):
    tm_count, chan_count, blocks, per, inputs = sizes
    groups = LANES // inputs
    channels = per // 2
    if places is None:
        got_ref, (out_ref, token_ref) = refs[0], refs[-2:]
    else:
        out_ref, token_ref, got_ref, sems = refs[-4:]

    @pl.when(pl.program_id(0) == 0)
    def _():
        token_ref[...] = jnp.zeros_like(token_ref)

    @pl.when(pl.program_id(0) == 0)
    def _():
        copies = []
        for index, (base, rows, into) in enumerate(places or []):
            source = refs[index].at[:, pl.ds(base, rows), :]
            target = got_ref.at[:, pl.ds(into, rows), :]
            copies.append(pltpu.make_async_copy(source, target, sems.at[index]))
            copies[-1].start()
        for copy in copies:
            copy.wait()

    lane_group = lax.broadcasted_iota(jnp.int32, (blocks, LANES), 1) // inputs

    def piece(channel, time, chan, part):
        rows = pl.ds(part * channels + channel, blocks, stride=per)
        return got_ref[time * chan_count + chan, rows, :]

    def tile(channel, time, part, column):
        held = [piece(channel, time, column * groups + place, part) for place in range(groups)]
        made = []
        for group in range(groups):
            total = None
            for place in range(groups):
                turn = (place - group) * inputs % LANES
                value = pltpu.roll(held[place], turn, 1) if turn else held[place]
                total = value if total is None else jnp.where(lane_group == place, value, total)
            made.append(total)
        return jnp.concatenate(made, axis=0)

    def plane(channel, part):
        columns = []
        for column in range(chan_count // groups):
            columns.append(
                jnp.concatenate([tile(channel, time, part, column) for time in range(tm_count)], axis=0)
            )
        return jnp.concatenate(columns, axis=1)

    dot = functools.partial(lax.dot_general, dimension_numbers=NN, preferred_element_type=jnp.float32)
    for sub in range(PAIR):
        channel = pl.program_id(0) * PAIR + sub
        real, imag = plane(channel, 0), plane(channel, 1)
        real_high, real_low = halves(real)
        imag_high, imag_low = halves(imag)
        high = jnp.concatenate([real_high, imag_high], axis=0)
        low = jnp.concatenate([real_low, imag_low], axis=0)
        turned_high = jnp.concatenate([-imag_high, real_high], axis=0)
        turned_low = jnp.concatenate([-imag_low, real_low], axis=0)
        high_t, low_t = high.T, low.T
        for which, (other_high, other_low) in enumerate([(high, low), (turned_high, turned_low)]):
            total = dot(high_t, other_high) + dot(high_t, other_low) + dot(low_t, other_high)
            out_ref[sub, 0, which] = total * scale


def correlate_chunk(pieces, held, start, owned, sizes, spectra):
    tm_count, chan_count, blocks, per, inputs = sizes
    channels = per // 2
    everyone = chan_count * inputs
    owners = tm_count * chan_count
    operands = [piece[0] for piece in pieces]
    places = [piece[1:] for piece in pieces]
    in_specs = [pl.BlockSpec(memory_space=pl.ANY)] * len(operands)
    limit = 60
    scratch = [
        pltpu.VMEM((owners, blocks * per, LANES), jnp.float32),
        pltpu.SemaphoreType.DMA((len(pieces),)),
    ]
    if len(pieces) == 1 and operands[0].shape[1] == blocks * per and per <= 8:
        places, scratch, limit = None, [], 40
        in_specs = [pl.BlockSpec(operands[0].shape, lambda c: (0, 0, 0))]
    aliases = {}
    if held is not None:
        aliases = {len(operands): 0}
        operands.append(held)
        in_specs.append(pl.BlockSpec(memory_space=pl.ANY))
    return pl.pallas_call(
        functools.partial(correlate_kernel, sizes, 1.0 / spectra, places),
        grid=(channels // PAIR,),
        in_specs=in_specs,
        out_specs=[
            pl.BlockSpec((PAIR, 1, 2, everyone, everyone), lambda c: (start // 2 // PAIR + c, start % 2, 0, 0, 0)),
            pl.BlockSpec((8, LANES), lambda c: (0, 0)),
        ],
        out_shape=[
            jax.ShapeDtypeStruct((owned // 2, 2, 2, everyone, everyone), jnp.float32),
            jax.ShapeDtypeStruct((8, LANES), jnp.float32),
        ],
        input_output_aliases=aliases,
        scratch_shapes=scratch,
        compiler_params=params(limit),
        cost_estimate=pl.CostEstimate(
            flops=6 * channels * 2 * everyone * everyone * 2 * spectra,
            bytes_accessed=channels * 8 * everyone * everyone + 4 * owners * blocks * per * LANES,
            transcendentals=0,
        ),
        name="correlate_chunk",
    )(*operands)


def chunk_plan(owned):
    unit = owned // 8
    if owned % 32 == 0:
        return [[(0, 2 * unit)], [(2 * unit + 1, 3 * unit), (4 * unit, 2 * unit)], [(1, unit)]]
    return [[(parity, owned // 2)] for parity in (0, 1)]


def phases(frame, owners, owned, segments):
    samples = np.arange(frame // 2)
    outer = 2.0 * np.pi * ((np.arange(owners)[:, None] * owned * samples) % frame) / frame
    outer = np.stack([np.cos(outer), np.sin(outer)]).astype(np.float32)
    scale = 1.0 / np.sqrt(float(frame))
    tables = {}
    for start, count in segments:
        channels = start + 2 * np.arange(count)
        inner = 2.0 * np.pi * ((channels[:, None] * samples) % frame) / frame
        cosine, sine = np.cos(inner) * scale, np.sin(inner) * scale
        first = np.concatenate([cosine, -sine]).astype(np.float32)
        second = np.concatenate([-sine, -cosine]).astype(np.float32)
        tables[start, count] = (first, second)
    return outer, tables


def body(voltages, fir_taps):
    inputs, samples = voltages.shape
    taps, frame = fir_taps.shape
    spec_dev = samples // frame
    tm_count, chan_count = lax.axis_size("tm"), lax.axis_size("chan")
    owners = tm_count * chan_count
    owned = frame // 2 // owners
    groups = LANES // inputs
    blocks = spec_dev // groups
    chunks = chunk_plan(owned)
    outer, tables = phases(frame, owners, owned, sum(chunks, []))
    split = blocks > LATE and len(chunks) > 2

    def exchange(value):
        return lax.all_to_all(value, AXES, split_axis=0, concat_axis=0, tiled=True)

    halo = passed_along(voltages[:, samples - (taps - 1) * frame :], "tm", 1)
    if split:
        ahead = first_chunk(outer, *tables[chunks[0][0]], voltages, fir_taps, blocks, groups)
        ahead, halo = lax.optimization_barrier((ahead, halo))
    parts = filtered_parts(voltages, halo, fir_taps, blocks, groups)

    def transformed(segment, count, made, base, rows, token):
        return dft_chunk(
            outer, *tables[segment], *parts[segment[0] % 2], count, made, base, rows, token
        )

    pieces = {segment: [] for segment in sum(chunks, [])}
    out, token = None, None

    def correlate(segments):
        nonlocal out, token
        for segment in segments:
            start, count = segment
            sizes = (tm_count, chan_count, blocks, 2 * count, inputs)
            out, token = correlate_chunk(
                pieces[segment], out, start, owned, sizes, tm_count * spec_dev
            )

    payloads, layouts = [], []
    for index, chunk in enumerate(chunks):
        if index == 0 and split:
            (segment,) = chunk
            per = 2 * segment[1]
            pieces[segment].append((exchange(ahead), 0, (blocks - LATE) * per, LATE * per))
            continue
        plan = [(segment, blocks) for segment in chunk]
        if index == 1 and split:
            plan.append((chunks[0][0], LATE))
        rows = sum(2 * segment[1] * count for segment, count in plan)
        made, base, places = None, 0, []
        for segment, count in plan:
            made = transformed(segment, count, made, base, rows, token)
            places.append((segment, base, 2 * segment[1] * count))
            base += 2 * segment[1] * count
        payloads.append(made)
        layouts.append(places)
    payloads = lax.optimization_barrier(tuple(payloads))
    for made, places in zip(payloads, layouts):
        got = exchange(made)
        for segment, base, more in places:
            pieces[segment].append((got, base, more, 0))
    correlate(sum(chunks, []))
    return out.reshape(owned, 2, chan_count * inputs, chan_count * inputs)


def solution(mesh):
    placed = (P("chan", "tm"), P())
    return jax.shard_map(
        body,
        mesh=mesh,
        in_specs=placed,
        out_specs=P(("tm", "chan"), None, None, None),
        check_vma=False,
    )
```

```python
import functools
import math

import jax
import jax.numpy as jnp
import numpy as np
from jax import lax
from jax.experimental import pallas as pl
from jax.experimental.pallas import tpu as pltpu
from jax.sharding import PartitionSpec as P

LANES = 128
AXES = ("tm", "chan")
PAIR = 2
WIDE = 2
LATE = 6
NT = (((1,), (1,)), ((), ()))
NN = (((1,), (0,)), ((), ()))


def params(mib):
    return pltpu.CompilerParams(vmem_limit_bytes=mib << 20)


def halves(value):
    high = value.astype(jnp.bfloat16)
    low = (value - high.astype(jnp.float32)).astype(jnp.bfloat16)
    return high, low


def passed_along(value, axis, steps):
    count = lax.axis_size(axis)
    first, last = (max(0, -steps), min(count, count - steps))
    return lax.ppermute(value, axis, [(source, source + steps) for source in range(first, last)])


def weighted(frames, weights):
    total = frames[0] * weights[0]
    for frame, weight in zip(frames[1:], weights[1:]):
        total = total + frame * weight
    return total


def folded(left, right):
    return halves(left + right) + halves(left - right)


def filter_kernel(blocks, groups, taps, volt_ref, halo_ref, fir_ref, *out_refs):
    rows = volt_ref.shape[0]
    frame = fir_ref.shape[1]
    edge = taps - 1
    width = 2 * LANES

    def columns(column, carry):
        begins = [pl.multiple_of(column * width, width), pl.multiple_of(column * width + frame // 2, width)]
        here = pl.ds(begins[0], width)
        weights = [
            [jnp.broadcast_to(fir_ref[tap : tap + 1, pl.ds(begin, width)], (rows, width)) for tap in range(taps)]
            for begin in begins
        ]

        def step(spec, past):
            now = [volt_ref[:, pl.ds(pl.multiple_of(spec * frame + begin, width), width)] for begin in begins]
            sides = [weighted((now[k],) + past[k], weights[k]) for k in range(2)]
            block, group = lax.rem(spec, blocks), lax.div(spec, blocks)
            for ref, value in zip(out_refs, folded(*sides)):
                ref[block, group, :, here] = value
            return tuple((now[k],) + past[k][:-1] for k in range(2))

        past = tuple(
            tuple(
                halo_ref[:, pl.ds(pl.multiple_of((edge - 1 - k) * frame + begin, width), width)]
                for k in range(edge)
            )
            for begin in begins
        )
        lax.fori_loop(0, blocks * groups, step, past, unroll=4)
        return carry

    lax.fori_loop(0, frame // 2 // width, columns, 0)


def filtered_parts(voltages, halo, fir_taps, blocks, groups):
    inputs, samples = voltages.shape
    taps, frame = fir_taps.shape
    rows = 16
    shape = jax.ShapeDtypeStruct((blocks, groups, inputs, frame // 2), jnp.bfloat16)
    out_spec = pl.BlockSpec((blocks, groups, rows, frame // 2), lambda g: (0, 0, g, 0))
    made = pl.pallas_call(
        functools.partial(filter_kernel, blocks, groups, taps),
        grid=(inputs // rows,),
        in_specs=[
            pl.BlockSpec((rows, samples), lambda g: (g, 0)),
            pl.BlockSpec((rows, halo.shape[1]), lambda g: (g, 0)),
            pl.BlockSpec((taps, frame), lambda g: (0, 0)),
        ],
        out_specs=[out_spec] * 4,
        out_shape=[shape] * 4,
        compiler_params=params(60),
        cost_estimate=pl.CostEstimate(
            flops=8000 * inputs * samples, bytes_accessed=8 * inputs * samples, transcendentals=0
        ),
        name="polyphase_filter",
    )(voltages, halo, fir_taps)
    made = [part.reshape(blocks * groups * inputs, frame // 2) for part in made]
    return made[:2], made[2:]


def fill_table(owners, per, outer_ref, first_ref, second_ref, high_ref, low_ref):
    many = 16 // math.gcd(per, 16)

    def rows(step, carry):
        parts = []
        for extra in range(many):
            owner = step * many + extra
            cosine = outer_ref[0, pl.ds(owner, 1), :]
            sine = outer_ref[1, pl.ds(owner, 1), :]
            parts.append(first_ref[...] * cosine + second_ref[...] * sine)
        value = parts[0] if many == 1 else jnp.concatenate(parts, axis=0)
        high, low = halves(value)
        at = pl.ds(pl.multiple_of(step * many * per, many * per), many * per)
        high_ref[at, :] = high
        low_ref[at, :] = low
        return carry

    lax.fori_loop(0, owners // many, rows, 0)


def transform(owners, per, table_high, table_low, high, low, out_ref):
    dot = functools.partial(lax.dot_general, dimension_numbers=NT, preferred_element_type=jnp.float32)
    total = dot(table_high[...], high) + dot(table_high[...], low) + dot(table_low[...], high)
    for block in range(high.shape[0] // LANES):
        part = total[:, block * LANES : (block + 1) * LANES]
        out_ref[:, block * per : (block + 1) * per, :] = part.reshape(owners, per, LANES)


def dft_kernel(owners, per, outer_ref, first_ref, second_ref, high_ref, low_ref, *rest):
    out_ref, th_ref, tl_ref = rest[-3:]

    @pl.when(pl.program_id(0) == 0)
    def _():
        fill_table(owners, per, outer_ref, first_ref, second_ref, th_ref, tl_ref)

    transform(owners, per, th_ref, tl_ref, high_ref[...], low_ref[...], out_ref)


def dft_chunk(outer, first, second, high, low, blocks, held, base, total_rows, token=None):
    per, frame = first.shape
    owners = outer.shape[1]
    wide = 2 * WIDE if blocks % (2 * WIDE) == 0 and base % (2 * WIDE * per) == 0 else WIDE
    rows = wide * LANES
    assert base % (wide * per) == 0
    skip = base // (wide * per)
    const = lambda b: (0, 0)
    operands = [outer, first, second, high, low]
    in_specs = [
        pl.BlockSpec((2, owners, frame), lambda b: (0, 0, 0)),
        pl.BlockSpec((per, frame), const),
        pl.BlockSpec((per, frame), const),
        pl.BlockSpec((rows, frame), lambda b: (b, 0)),
        pl.BlockSpec((rows, frame), lambda b: (b, 0)),
    ]
    aliases = {}
    if held is not None:
        operands.append(held)
        in_specs.append(pl.BlockSpec(memory_space=pl.ANY))
        aliases = {5: 0}
    if token is not None:
        operands.append(token)
        in_specs.append(pl.BlockSpec(memory_space=pl.ANY))
    return pl.pallas_call(
        functools.partial(dft_kernel, owners, per),
        grid=(blocks // wide,),
        in_specs=in_specs,
        out_specs=pl.BlockSpec((owners, wide * per, LANES), lambda b: (0, skip + b, 0)),
        out_shape=jax.ShapeDtypeStruct((owners, total_rows, LANES), jnp.float32),
        input_output_aliases=aliases,
        scratch_shapes=[
            pltpu.VMEM((owners * per, frame), jnp.bfloat16),
            pltpu.VMEM((owners * per, frame), jnp.bfloat16),
        ],
        compiler_params=params(60),
        cost_estimate=pl.CostEstimate(
            flops=60 * owners * per * frame * blocks * LANES,
            bytes_accessed=4 * blocks * LANES * frame + 4 * owners * blocks * per * LANES,
            transcendentals=0,
        ),
        name="dft_chunk",
    )(*operands)


def first_kernel(owners, per, taps, groups, *refs):
    now = refs[:groups]
    fir_ref, outer_ref, first_ref, second_ref, out_ref = refs[groups : groups + 5]
    th_ref, tl_ref, past_ref, high_ref, low_ref = refs[groups + 5 :]
    inputs = now[0].shape[0]
    frame = fir_ref.shape[1]
    edge = taps - 1
    pair = pl.program_id(0)
    ahead = pl.cdiv(edge, WIDE)

    @pl.when(pair == 0)
    def _():
        fill_table(owners, per, outer_ref, first_ref, second_ref, th_ref, tl_ref)

    @pl.when(pair < ahead)
    def _():
        @pl.when(pair > 0)
        def _():
            for k in range(edge - WIDE):
                past_ref[k] = past_ref[k + WIDE]

        for group in range(groups):
            for k in range(WIDE):
                past_ref[edge - WIDE + k, group] = now[group][:, k * frame : (k + 1) * frame]

    @pl.when(pair >= ahead)
    def _():
        rows = 16
        width = 2 * LANES

        def columns(column, carry):
            begins = [
                pl.multiple_of(column * width, width),
                pl.multiple_of(column * width + frame // 2, width),
            ]
            weights = [
                [
                    jnp.broadcast_to(fir_ref[tap : tap + 1, pl.ds(begin, width)], (rows, width))
                    for tap in range(taps)
                ]
                for begin in begins
            ]
            for group in range(groups):
                for start in range(0, inputs, rows):
                    at = pl.ds(start, rows)
                    sums = [None] * WIDE
                    for begin, weight in zip(begins, weights):
                        here = pl.ds(begin, width)
                        frames = [past_ref[k, group, at, here] for k in range(edge)]
                        for spec in range(WIDE):
                            frames.append(
                                now[group][at, pl.ds(pl.multiple_of(spec * frame + begin, width), width)]
                            )
                        for spec in range(WIDE):
                            total = weighted([frames[edge + spec - tap] for tap in range(taps)], weight)
                            sums[spec] = total if sums[spec] is None else sums[spec] + total
                        for k in range(edge):
                            past_ref[k, group, at, here] = frames[WIDE + k]
                    for spec in range(WIDE):
                        high, low = halves(sums[spec])
                        place = pl.ds(spec * LANES + group * inputs + start, rows)
                        high_ref[place, pl.ds(begins[0], width)] = high
                        low_ref[place, pl.ds(begins[0], width)] = low
            return carry

        lax.fori_loop(0, frame // 2 // width, columns, 0)
        transform(owners, per, th_ref, tl_ref, high_ref[...], low_ref[...], out_ref)


def first_chunk(outer, first, second, voltages, fir_taps, blocks, groups):
    per, half = first.shape
    owners = outer.shape[1]
    inputs, samples = voltages.shape
    taps, frame = fir_taps.shape
    kept = blocks - LATE
    const = lambda b: (0, 0)

    ahead = pl.cdiv(taps - 1, WIDE)

    def now_map(group):
        return lambda b: (0, (group * blocks + LATE) // WIDE - ahead + b)

    return pl.pallas_call(
        functools.partial(first_kernel, owners, per, taps, groups),
        grid=(kept // WIDE + ahead,),
        in_specs=[pl.BlockSpec((inputs, WIDE * frame), now_map(g)) for g in range(groups)]
        + [
            pl.BlockSpec((taps, frame), const),
            pl.BlockSpec((2, owners, half), lambda b: (0, 0, 0)),
            pl.BlockSpec((per, half), const),
            pl.BlockSpec((per, half), const),
        ],
        out_specs=pl.BlockSpec((owners, WIDE * per, LANES), lambda b: (0, jnp.maximum(b - ahead, 0), 0)),
        out_shape=jax.ShapeDtypeStruct((owners, kept * per, LANES), jnp.float32),
        scratch_shapes=[
            pltpu.VMEM((owners * per, half), jnp.bfloat16),
            pltpu.VMEM((owners * per, half), jnp.bfloat16),
            pltpu.VMEM((taps - 1, groups, inputs, frame), jnp.float32),
            pltpu.VMEM((WIDE * LANES, half), jnp.bfloat16),
            pltpu.VMEM((WIDE * LANES, half), jnp.bfloat16),
        ],
        compiler_params=params(60),
        cost_estimate=pl.CostEstimate(
            flops=6 * owners * per * half * kept * LANES,
            bytes_accessed=4 * inputs * samples,
            transcendentals=0,
        ),
        name="first_chunk",
    )(*([voltages] * groups), fir_taps, outer, first, second)


def correlate_kernel(sizes, scale, places, *refs):
    tm_count, chan_count, blocks, per, inputs = sizes
    groups = LANES // inputs
    channels = per // 2
    if places is None:
        got_ref, (out_ref, token_ref) = refs[0], refs[-2:]
    else:
        out_ref, token_ref, got_ref, sems = refs[-4:]

    @pl.when(pl.program_id(0) == 0)
    def _():
        token_ref[...] = jnp.zeros_like(token_ref)

    @pl.when(pl.program_id(0) == 0)
    def _():
        copies = []
        for index, (base, rows, into) in enumerate(places or []):
            source = refs[index].at[:, pl.ds(base, rows), :]
            target = got_ref.at[:, pl.ds(into, rows), :]
            copies.append(pltpu.make_async_copy(source, target, sems.at[index]))
            copies[-1].start()
        for copy in copies:
            copy.wait()

    lane_group = lax.broadcasted_iota(jnp.int32, (blocks, LANES), 1) // inputs

    def piece(channel, time, chan, part):
        rows = pl.ds(part * channels + channel, blocks, stride=per)
        return got_ref[time * chan_count + chan, rows, :]

    def tile(channel, time, part, column):
        held = [piece(channel, time, column * groups + place, part) for place in range(groups)]
        made = []
        for group in range(groups):
            total = None
            for place in range(groups):
                turn = (place - group) * inputs % LANES
                value = pltpu.roll(held[place], turn, 1) if turn else held[place]
                total = value if total is None else jnp.where(lane_group == place, value, total)
            made.append(total)
        return jnp.concatenate(made, axis=0)

    def plane(channel, part):
        columns = []
        for column in range(chan_count // groups):
            columns.append(
                jnp.concatenate([tile(channel, time, part, column) for time in range(tm_count)], axis=0)
            )
        return jnp.concatenate(columns, axis=1)

    dot = functools.partial(lax.dot_general, dimension_numbers=NN, preferred_element_type=jnp.float32)
    for sub in range(PAIR):
        channel = pl.program_id(0) * PAIR + sub
        real, imag = plane(channel, 0), plane(channel, 1)
        real_high, real_low = halves(real)
        imag_high, imag_low = halves(imag)
        high = jnp.concatenate([real_high, imag_high], axis=0)
        low = jnp.concatenate([real_low, imag_low], axis=0)
        turned_high = jnp.concatenate([-imag_high, real_high], axis=0)
        turned_low = jnp.concatenate([-imag_low, real_low], axis=0)
        high_t, low_t = high.T, low.T
        for which, (other_high, other_low) in enumerate([(high, low), (turned_high, turned_low)]):
            total = dot(high_t, other_high) + dot(high_t, other_low) + dot(low_t, other_high)
            out_ref[sub, 0, which] = total * scale


def correlate_chunk(pieces, held, start, owned, sizes, spectra):
    tm_count, chan_count, blocks, per, inputs = sizes
    channels = per // 2
    everyone = chan_count * inputs
    owners = tm_count * chan_count
    operands = [piece[0] for piece in pieces]
    places = [piece[1:] for piece in pieces]
    in_specs = [pl.BlockSpec(memory_space=pl.ANY)] * len(operands)
    limit = 60
    scratch = [
        pltpu.VMEM((owners, blocks * per, LANES), jnp.float32),
        pltpu.SemaphoreType.DMA((len(pieces),)),
    ]
    if len(pieces) == 1 and operands[0].shape[1] == blocks * per and per <= 8:
        places, scratch, limit = None, [], 40
        in_specs = [pl.BlockSpec(operands[0].shape, lambda c: (0, 0, 0))]
    aliases = {}
    if held is not None:
        aliases = {len(operands): 0}
        operands.append(held)
        in_specs.append(pl.BlockSpec(memory_space=pl.ANY))
    return pl.pallas_call(
        functools.partial(correlate_kernel, sizes, 1.0 / spectra, places),
        grid=(channels // PAIR,),
        in_specs=in_specs,
        out_specs=[
            pl.BlockSpec((PAIR, 1, 2, everyone, everyone), lambda c: (start // 2 // PAIR + c, start % 2, 0, 0, 0)),
            pl.BlockSpec((8, LANES), lambda c: (0, 0)),
        ],
        out_shape=[
            jax.ShapeDtypeStruct((owned // 2, 2, 2, everyone, everyone), jnp.float32),
            jax.ShapeDtypeStruct((8, LANES), jnp.float32),
        ],
        input_output_aliases=aliases,
        scratch_shapes=scratch,
        compiler_params=params(limit),
        cost_estimate=pl.CostEstimate(
            flops=6 * channels * 2 * everyone * everyone * 2 * spectra,
            bytes_accessed=channels * 8 * everyone * everyone + 4 * owners * blocks * per * LANES,
            transcendentals=0,
        ),
        name="correlate_chunk",
    )(*operands)


def chunk_plan(owned):
    unit = owned // 8
    if owned % 32 == 0:
        return [[(0, 2 * unit)], [(2 * unit + 1, 3 * unit), (4 * unit, 2 * unit)], [(1, unit)]]
    return [[(parity, owned // 2)] for parity in (0, 1)]


def phases(frame, owners, owned, segments):
    samples = np.arange(frame // 2)
    outer = 2.0 * np.pi * ((np.arange(owners)[:, None] * owned * samples) % frame) / frame
    outer = np.stack([np.cos(outer), np.sin(outer)]).astype(np.float32)
    scale = 1.0 / np.sqrt(float(frame))
    tables = {}
    for start, count in segments:
        channels = start + 2 * np.arange(count)
        inner = 2.0 * np.pi * ((channels[:, None] * samples) % frame) / frame
        cosine, sine = np.cos(inner) * scale, np.sin(inner) * scale
        first = np.concatenate([cosine, -sine]).astype(np.float32)
        second = np.concatenate([-sine, -cosine]).astype(np.float32)
        tables[start, count] = (first, second)
    return outer, tables


def body(voltages, fir_taps):
    inputs, samples = voltages.shape
    taps, frame = fir_taps.shape
    spec_dev = samples // frame
    tm_count, chan_count = lax.axis_size("tm"), lax.axis_size("chan")
    owners = tm_count * chan_count
    owned = frame // 2 // owners
    groups = LANES // inputs
    blocks = spec_dev // groups
    chunks = chunk_plan(owned)
    outer, tables = phases(frame, owners, owned, sum(chunks, []))
    split = blocks > LATE and len(chunks) > 2

    def exchange(value):
        return lax.all_to_all(value, AXES, split_axis=0, concat_axis=0, tiled=True)

    halo = passed_along(voltages[:, samples - (taps - 1) * frame :], "tm", 1)
    if split:
        ahead = first_chunk(outer, *tables[chunks[0][0]], voltages, fir_taps, blocks, groups)
    parts = filtered_parts(voltages, halo, fir_taps, blocks, groups)

    def transformed(segment, count, made, base, rows, token):
        return dft_chunk(
            outer, *tables[segment], *parts[segment[0] % 2], count, made, base, rows, token
        )

    pieces = {segment: [] for segment in sum(chunks, [])}
    out, token = None, None

    def correlate(segments):
        nonlocal out, token
        for segment in segments:
            start, count = segment
            sizes = (tm_count, chan_count, blocks, 2 * count, inputs)
            out, token = correlate_chunk(
                pieces[segment], out, start, owned, sizes, tm_count * spec_dev
            )

    payloads, layouts = [], []
    for index, chunk in enumerate(chunks):
        if index == 0 and split:
            (segment,) = chunk
            per = 2 * segment[1]
            pieces[segment].append((exchange(ahead), 0, (blocks - LATE) * per, LATE * per))
            continue
        plan = [(segment, blocks) for segment in chunk]
        if index == 1 and split:
            plan.append((chunks[0][0], LATE))
        rows = sum(2 * segment[1] * count for segment, count in plan)
        made, base, places = None, 0, []
        for segment, count in plan:
            made = transformed(segment, count, made, base, rows, token)
            places.append((segment, base, 2 * segment[1] * count))
            base += 2 * segment[1] * count
        payloads.append(made)
        layouts.append(places)
    payloads = lax.optimization_barrier(tuple(payloads))
    for made, places in zip(payloads, layouts):
        got = exchange(made)
        for segment, base, more in places:
            pieces[segment].append((got, base, more, 0))
    correlate(sum(chunks, []))
    return out.reshape(owned, 2, chan_count * inputs, chan_count * inputs)


def solution(mesh):
    placed = (P("chan", "tm"), P())
    return jax.shard_map(
        body,
        mesh=mesh,
        in_specs=placed,
        out_specs=P(("tm", "chan"), None, None, None),
        check_vma=False,
    )
```

```python
import functools
import math

import jax
import jax.numpy as jnp
import numpy as np
from jax import lax
from jax.experimental import pallas as pl
from jax.experimental.pallas import tpu as pltpu
from jax.sharding import PartitionSpec as P

LANES = 128
AXES = ("tm", "chan")
PAIR = 2
WIDE = 2
LATE = 10
NT = (((1,), (1,)), ((), ()))
NN = (((1,), (0,)), ((), ()))


def params(mib):
    return pltpu.CompilerParams(vmem_limit_bytes=mib << 20)


def halves(value):
    high = value.astype(jnp.bfloat16)
    low = (value - high.astype(jnp.float32)).astype(jnp.bfloat16)
    return high, low


def passed_along(value, axis, steps):
    count = lax.axis_size(axis)
    first, last = (max(0, -steps), min(count, count - steps))
    return lax.ppermute(value, axis, [(source, source + steps) for source in range(first, last)])


def weighted(frames, weights):
    total = frames[0] * weights[0]
    for frame, weight in zip(frames[1:], weights[1:]):
        total = total + frame * weight
    return total


def folded(left, right):
    return halves(left + right) + halves(left - right)


def filter_kernel(blocks, groups, taps, volt_ref, halo_ref, fir_ref, *out_refs):
    rows = volt_ref.shape[0]
    frame = fir_ref.shape[1]
    edge = taps - 1
    width = 2 * LANES

    def columns(column, carry):
        begins = [pl.multiple_of(column * width, width), pl.multiple_of(column * width + frame // 2, width)]
        here = pl.ds(begins[0], width)
        weights = [
            [jnp.broadcast_to(fir_ref[tap : tap + 1, pl.ds(begin, width)], (rows, width)) for tap in range(taps)]
            for begin in begins
        ]

        def step(spec, past):
            now = [volt_ref[:, pl.ds(pl.multiple_of(spec * frame + begin, width), width)] for begin in begins]
            sides = [weighted((now[k],) + past[k], weights[k]) for k in range(2)]
            block, group = lax.rem(spec, blocks), lax.div(spec, blocks)
            for ref, value in zip(out_refs, folded(*sides)):
                ref[block, group, :, here] = value
            return tuple((now[k],) + past[k][:-1] for k in range(2))

        past = tuple(
            tuple(
                halo_ref[:, pl.ds(pl.multiple_of((edge - 1 - k) * frame + begin, width), width)]
                for k in range(edge)
            )
            for begin in begins
        )
        lax.fori_loop(0, blocks * groups, step, past, unroll=4)
        return carry

    lax.fori_loop(0, frame // 2 // width, columns, 0)


def filtered_parts(voltages, halo, fir_taps, blocks, groups):
    inputs, samples = voltages.shape
    taps, frame = fir_taps.shape
    rows = 16
    shape = jax.ShapeDtypeStruct((blocks, groups, inputs, frame // 2), jnp.bfloat16)
    out_spec = pl.BlockSpec((blocks, groups, rows, frame // 2), lambda g: (0, 0, g, 0))
    made = pl.pallas_call(
        functools.partial(filter_kernel, blocks, groups, taps),
        grid=(inputs // rows,),
        in_specs=[
            pl.BlockSpec((rows, samples), lambda g: (g, 0)),
            pl.BlockSpec((rows, halo.shape[1]), lambda g: (g, 0)),
            pl.BlockSpec((taps, frame), lambda g: (0, 0)),
        ],
        out_specs=[out_spec] * 4,
        out_shape=[shape] * 4,
        compiler_params=params(60),
        cost_estimate=pl.CostEstimate(
            flops=8000 * inputs * samples, bytes_accessed=8 * inputs * samples, transcendentals=0
        ),
        name="polyphase_filter",
    )(voltages, halo, fir_taps)
    made = [part.reshape(blocks * groups * inputs, frame // 2) for part in made]
    return made[:2], made[2:]


def fill_table(owners, per, outer_ref, first_ref, second_ref, high_ref, low_ref):
    many = 16 // math.gcd(per, 16)

    def rows(step, carry):
        parts = []
        for extra in range(many):
            owner = step * many + extra
            cosine = outer_ref[0, pl.ds(owner, 1), :]
            sine = outer_ref[1, pl.ds(owner, 1), :]
            parts.append(first_ref[...] * cosine + second_ref[...] * sine)
        value = parts[0] if many == 1 else jnp.concatenate(parts, axis=0)
        high, low = halves(value)
        at = pl.ds(pl.multiple_of(step * many * per, many * per), many * per)
        high_ref[at, :] = high
        low_ref[at, :] = low
        return carry

    lax.fori_loop(0, owners // many, rows, 0)


def transform(owners, per, table_high, table_low, high, low, out_ref):
    dot = functools.partial(lax.dot_general, dimension_numbers=NT, preferred_element_type=jnp.float32)
    total = dot(table_high[...], high) + dot(table_high[...], low) + dot(table_low[...], high)
    for block in range(high.shape[0] // LANES):
        part = total[:, block * LANES : (block + 1) * LANES]
        out_ref[:, block * per : (block + 1) * per, :] = part.reshape(owners, per, LANES)


def dft_kernel(owners, per, outer_ref, first_ref, second_ref, high_ref, low_ref, *rest):
    out_ref, th_ref, tl_ref = rest[-3:]

    @pl.when(pl.program_id(0) == 0)
    def _():
        fill_table(owners, per, outer_ref, first_ref, second_ref, th_ref, tl_ref)

    transform(owners, per, th_ref, tl_ref, high_ref[...], low_ref[...], out_ref)


def dft_chunk(outer, first, second, high, low, blocks, held, base, total_rows, token=None):
    per, frame = first.shape
    owners = outer.shape[1]
    wide = 2 * WIDE if blocks % (2 * WIDE) == 0 and base % (2 * WIDE * per) == 0 else WIDE
    rows = wide * LANES
    assert base % (wide * per) == 0
    skip = base // (wide * per)
    const = lambda b: (0, 0)
    operands = [outer, first, second, high, low]
    in_specs = [
        pl.BlockSpec((2, owners, frame), lambda b: (0, 0, 0)),
        pl.BlockSpec((per, frame), const),
        pl.BlockSpec((per, frame), const),
        pl.BlockSpec((rows, frame), lambda b: (b, 0)),
        pl.BlockSpec((rows, frame), lambda b: (b, 0)),
    ]
    aliases = {}
    if held is not None:
        operands.append(held)
        in_specs.append(pl.BlockSpec(memory_space=pl.ANY))
        aliases = {5: 0}
    if token is not None:
        operands.append(token)
        in_specs.append(pl.BlockSpec(memory_space=pl.ANY))
    return pl.pallas_call(
        functools.partial(dft_kernel, owners, per),
        grid=(blocks // wide,),
        in_specs=in_specs,
        out_specs=pl.BlockSpec((owners, wide * per, LANES), lambda b: (0, skip + b, 0)),
        out_shape=jax.ShapeDtypeStruct((owners, total_rows, LANES), jnp.float32),
        input_output_aliases=aliases,
        scratch_shapes=[
            pltpu.VMEM((owners * per, frame), jnp.bfloat16),
            pltpu.VMEM((owners * per, frame), jnp.bfloat16),
        ],
        compiler_params=params(60),
        cost_estimate=pl.CostEstimate(
            flops=60 * owners * per * frame * blocks * LANES,
            bytes_accessed=4 * blocks * LANES * frame + 4 * owners * blocks * per * LANES,
            transcendentals=0,
        ),
        name="dft_chunk",
    )(*operands)


def first_kernel(owners, per, taps, groups, *refs):
    now = refs[:groups]
    fir_ref, outer_ref, first_ref, second_ref, out_ref = refs[groups : groups + 5]
    th_ref, tl_ref, past_ref, high_ref, low_ref = refs[groups + 5 :]
    inputs = now[0].shape[0]
    frame = fir_ref.shape[1]
    edge = taps - 1
    pair = pl.program_id(0)
    ahead = pl.cdiv(edge, WIDE)

    @pl.when(pair == 0)
    def _():
        fill_table(owners, per, outer_ref, first_ref, second_ref, th_ref, tl_ref)

    @pl.when(pair < ahead)
    def _():
        @pl.when(pair > 0)
        def _():
            for k in range(edge - WIDE):
                past_ref[k] = past_ref[k + WIDE]

        for group in range(groups):
            for k in range(WIDE):
                past_ref[edge - WIDE + k, group] = now[group][:, k * frame : (k + 1) * frame]

    @pl.when(pair >= ahead)
    def _():
        rows = 16
        width = 2 * LANES

        def columns(column, carry):
            begins = [
                pl.multiple_of(column * width, width),
                pl.multiple_of(column * width + frame // 2, width),
            ]
            weights = [
                [
                    jnp.broadcast_to(fir_ref[tap : tap + 1, pl.ds(begin, width)], (rows, width))
                    for tap in range(taps)
                ]
                for begin in begins
            ]
            for group in range(groups):
                for start in range(0, inputs, rows):
                    at = pl.ds(start, rows)
                    sums = [None] * WIDE
                    for begin, weight in zip(begins, weights):
                        here = pl.ds(begin, width)
                        frames = [past_ref[k, group, at, here] for k in range(edge)]
                        for spec in range(WIDE):
                            frames.append(
                                now[group][at, pl.ds(pl.multiple_of(spec * frame + begin, width), width)]
                            )
                        for spec in range(WIDE):
                            total = weighted([frames[edge + spec - tap] for tap in range(taps)], weight)
                            sums[spec] = total if sums[spec] is None else sums[spec] + total
                        for k in range(edge):
                            past_ref[k, group, at, here] = frames[WIDE + k]
                    for spec in range(WIDE):
                        high, low = halves(sums[spec])
                        place = pl.ds(spec * LANES + group * inputs + start, rows)
                        high_ref[place, pl.ds(begins[0], width)] = high
                        low_ref[place, pl.ds(begins[0], width)] = low
            return carry

        lax.fori_loop(0, frame // 2 // width, columns, 0)
        transform(owners, per, th_ref, tl_ref, high_ref[...], low_ref[...], out_ref)


def first_chunk(outer, first, second, voltages, fir_taps, blocks, groups):
    per, half = first.shape
    owners = outer.shape[1]
    inputs, samples = voltages.shape
    taps, frame = fir_taps.shape
    kept = blocks - LATE
    const = lambda b: (0, 0)

    ahead = pl.cdiv(taps - 1, WIDE)

    def now_map(group):
        return lambda b: (0, (group * blocks + LATE) // WIDE - ahead + b)

    return pl.pallas_call(
        functools.partial(first_kernel, owners, per, taps, groups),
        grid=(kept // WIDE + ahead,),
        in_specs=[pl.BlockSpec((inputs, WIDE * frame), now_map(g)) for g in range(groups)]
        + [
            pl.BlockSpec((taps, frame), const),
            pl.BlockSpec((2, owners, half), lambda b: (0, 0, 0)),
            pl.BlockSpec((per, half), const),
            pl.BlockSpec((per, half), const),
        ],
        out_specs=pl.BlockSpec((owners, WIDE * per, LANES), lambda b: (0, jnp.maximum(b - ahead, 0), 0)),
        out_shape=jax.ShapeDtypeStruct((owners, kept * per, LANES), jnp.float32),
        scratch_shapes=[
            pltpu.VMEM((owners * per, half), jnp.bfloat16),
            pltpu.VMEM((owners * per, half), jnp.bfloat16),
            pltpu.VMEM((taps - 1, groups, inputs, frame), jnp.float32),
            pltpu.VMEM((WIDE * LANES, half), jnp.bfloat16),
            pltpu.VMEM((WIDE * LANES, half), jnp.bfloat16),
        ],
        compiler_params=params(60),
        cost_estimate=pl.CostEstimate(
            flops=6 * owners * per * half * kept * LANES,
            bytes_accessed=4 * inputs * samples,
            transcendentals=0,
        ),
        name="first_chunk",
    )(*([voltages] * groups), fir_taps, outer, first, second)


def correlate_kernel(sizes, scale, places, *refs):
    tm_count, chan_count, blocks, per, inputs = sizes
    groups = LANES // inputs
    channels = per // 2
    if places is None:
        got_ref, (out_ref, token_ref) = refs[0], refs[-2:]
    else:
        out_ref, token_ref, got_ref, sems = refs[-4:]

    @pl.when(pl.program_id(0) == 0)
    def _():
        token_ref[...] = jnp.zeros_like(token_ref)

    @pl.when(pl.program_id(0) == 0)
    def _():
        copies = []
        for index, (base, rows, into) in enumerate(places or []):
            source = refs[index].at[:, pl.ds(base, rows), :]
            target = got_ref.at[:, pl.ds(into, rows), :]
            copies.append(pltpu.make_async_copy(source, target, sems.at[index]))
            copies[-1].start()
        for copy in copies:
            copy.wait()

    lane_group = lax.broadcasted_iota(jnp.int32, (blocks, LANES), 1) // inputs

    def piece(channel, time, chan, part):
        rows = pl.ds(part * channels + channel, blocks, stride=per)
        return got_ref[time * chan_count + chan, rows, :]

    def tile(channel, time, part, column):
        held = [piece(channel, time, column * groups + place, part) for place in range(groups)]
        made = []
        for group in range(groups):
            total = None
            for place in range(groups):
                turn = (place - group) * inputs % LANES
                value = pltpu.roll(held[place], turn, 1) if turn else held[place]
                total = value if total is None else jnp.where(lane_group == place, value, total)
            made.append(total)
        return jnp.concatenate(made, axis=0)

    def plane(channel, part):
        columns = []
        for column in range(chan_count // groups):
            columns.append(
                jnp.concatenate([tile(channel, time, part, column) for time in range(tm_count)], axis=0)
            )
        return jnp.concatenate(columns, axis=1)

    dot = functools.partial(lax.dot_general, dimension_numbers=NN, preferred_element_type=jnp.float32)
    for sub in range(PAIR):
        channel = pl.program_id(0) * PAIR + sub
        real, imag = plane(channel, 0), plane(channel, 1)
        real_high, real_low = halves(real)
        imag_high, imag_low = halves(imag)
        high = jnp.concatenate([real_high, imag_high], axis=0)
        low = jnp.concatenate([real_low, imag_low], axis=0)
        turned_high = jnp.concatenate([-imag_high, real_high], axis=0)
        turned_low = jnp.concatenate([-imag_low, real_low], axis=0)
        high_t, low_t = high.T, low.T
        for which, (other_high, other_low) in enumerate([(high, low), (turned_high, turned_low)]):
            total = dot(high_t, other_high) + dot(high_t, other_low) + dot(low_t, other_high)
            out_ref[sub, 0, which] = total * scale


def correlate_chunk(pieces, held, start, owned, sizes, spectra):
    tm_count, chan_count, blocks, per, inputs = sizes
    channels = per // 2
    everyone = chan_count * inputs
    owners = tm_count * chan_count
    operands = [piece[0] for piece in pieces]
    places = [piece[1:] for piece in pieces]
    in_specs = [pl.BlockSpec(memory_space=pl.ANY)] * len(operands)
    limit = 60
    scratch = [
        pltpu.VMEM((owners, blocks * per, LANES), jnp.float32),
        pltpu.SemaphoreType.DMA((len(pieces),)),
    ]
    if len(pieces) == 1 and operands[0].shape[1] == blocks * per and per <= 8:
        places, scratch, limit = None, [], 40
        in_specs = [pl.BlockSpec(operands[0].shape, lambda c: (0, 0, 0))]
    aliases = {}
    if held is not None:
        aliases = {len(operands): 0}
        operands.append(held)
        in_specs.append(pl.BlockSpec(memory_space=pl.ANY))
    return pl.pallas_call(
        functools.partial(correlate_kernel, sizes, 1.0 / spectra, places),
        grid=(channels // PAIR,),
        in_specs=in_specs,
        out_specs=[
            pl.BlockSpec((PAIR, 1, 2, everyone, everyone), lambda c: (start // 2 // PAIR + c, start % 2, 0, 0, 0)),
            pl.BlockSpec((8, LANES), lambda c: (0, 0)),
        ],
        out_shape=[
            jax.ShapeDtypeStruct((owned // 2, 2, 2, everyone, everyone), jnp.float32),
            jax.ShapeDtypeStruct((8, LANES), jnp.float32),
        ],
        input_output_aliases=aliases,
        scratch_shapes=scratch,
        compiler_params=params(limit),
        cost_estimate=pl.CostEstimate(
            flops=6 * channels * 2 * everyone * everyone * 2 * spectra,
            bytes_accessed=channels * 8 * everyone * everyone + 4 * owners * blocks * per * LANES,
            transcendentals=0,
        ),
        name="correlate_chunk",
    )(*operands)


def chunk_plan(owned):
    unit = owned // 8
    if owned % 32 == 0:
        return [[(0, 4 * unit)], [(2 * unit + 1, 3 * unit)], [(1, unit)]]
    return [[(parity, owned // 2)] for parity in (0, 1)]


def phases(frame, owners, owned, segments):
    samples = np.arange(frame // 2)
    outer = 2.0 * np.pi * ((np.arange(owners)[:, None] * owned * samples) % frame) / frame
    outer = np.stack([np.cos(outer), np.sin(outer)]).astype(np.float32)
    scale = 1.0 / np.sqrt(float(frame))
    tables = {}
    for start, count in segments:
        channels = start + 2 * np.arange(count)
        inner = 2.0 * np.pi * ((channels[:, None] * samples) % frame) / frame
        cosine, sine = np.cos(inner) * scale, np.sin(inner) * scale
        first = np.concatenate([cosine, -sine]).astype(np.float32)
        second = np.concatenate([-sine, -cosine]).astype(np.float32)
        tables[start, count] = (first, second)
    return outer, tables


def body(voltages, fir_taps):
    inputs, samples = voltages.shape
    taps, frame = fir_taps.shape
    spec_dev = samples // frame
    tm_count, chan_count = lax.axis_size("tm"), lax.axis_size("chan")
    owners = tm_count * chan_count
    owned = frame // 2 // owners
    groups = LANES // inputs
    blocks = spec_dev // groups
    chunks = chunk_plan(owned)
    outer, tables = phases(frame, owners, owned, sum(chunks, []))
    split = blocks > LATE and len(chunks) > 2

    def exchange(value):
        return lax.all_to_all(value, AXES, split_axis=0, concat_axis=0, tiled=True)

    halo = passed_along(voltages[:, samples - (taps - 1) * frame :], "tm", 1)
    if split:
        ahead = first_chunk(outer, *tables[chunks[0][0]], voltages, fir_taps, blocks, groups)
    parts = filtered_parts(voltages, halo, fir_taps, blocks, groups)

    def transformed(segment, count, made, base, rows, token):
        return dft_chunk(
            outer, *tables[segment], *parts[segment[0] % 2], count, made, base, rows, token
        )

    pieces = {segment: [] for segment in sum(chunks, [])}
    out, token = None, None

    def correlate(segments):
        nonlocal out, token
        for segment in segments:
            start, count = segment
            sizes = (tm_count, chan_count, blocks, 2 * count, inputs)
            out, token = correlate_chunk(
                pieces[segment], out, start, owned, sizes, tm_count * spec_dev
            )

    payloads, layouts = [], []
    for index, chunk in enumerate(chunks):
        if index == 0 and split:
            (segment,) = chunk
            per = 2 * segment[1]
            pieces[segment].append((exchange(ahead), 0, (blocks - LATE) * per, LATE * per))
            continue
        plan = [(segment, blocks) for segment in chunk]
        if index == 1 and split:
            plan.append((chunks[0][0], LATE))
        rows = sum(2 * segment[1] * count for segment, count in plan)
        made, base, places = None, 0, []
        for segment, count in plan:
            made = transformed(segment, count, made, base, rows, token)
            places.append((segment, base, 2 * segment[1] * count))
            base += 2 * segment[1] * count
        payloads.append(made)
        layouts.append(places)
    payloads = lax.optimization_barrier(tuple(payloads))
    for made, places in zip(payloads, layouts):
        got = exchange(made)
        for segment, base, more in places:
            pieces[segment].append((got, base, more, 0))
    correlate(sum(chunks, []))
    return out.reshape(owned, 2, chan_count * inputs, chan_count * inputs)


def solution(mesh):
    placed = (P("chan", "tm"), P())
    return jax.shard_map(
        body,
        mesh=mesh,
        in_specs=placed,
        out_specs=P(("tm", "chan"), None, None, None),
        check_vma=False,
    )
```

```python
import functools
import math

import jax
import jax.numpy as jnp
import numpy as np
from jax import lax
from jax.experimental import pallas as pl
from jax.experimental.pallas import tpu as pltpu
from jax.sharding import PartitionSpec as P

LANES = 128
AXES = ("tm", "chan")
PAIR = 2
WIDE = 2
LATE = 10
NT = (((1,), (1,)), ((), ()))
NN = (((1,), (0,)), ((), ()))


def params(mib):
    return pltpu.CompilerParams(vmem_limit_bytes=mib << 20)


def halves(value):
    high = value.astype(jnp.bfloat16)
    low = (value - high.astype(jnp.float32)).astype(jnp.bfloat16)
    return high, low


def passed_along(value, axis, steps):
    count = lax.axis_size(axis)
    first, last = (max(0, -steps), min(count, count - steps))
    return lax.ppermute(value, axis, [(source, source + steps) for source in range(first, last)])


def weighted(frames, weights):
    total = frames[0] * weights[0]
    for frame, weight in zip(frames[1:], weights[1:]):
        total = total + frame * weight
    return total


def folded(left, right):
    return halves(left + right) + halves(left - right)


def filter_kernel(blocks, groups, taps, volt_ref, halo_ref, fir_ref, *out_refs):
    rows = volt_ref.shape[0]
    frame = fir_ref.shape[1]
    edge = taps - 1
    width = 2 * LANES

    def columns(column, carry):
        begins = [pl.multiple_of(column * width, width), pl.multiple_of(column * width + frame // 2, width)]
        here = pl.ds(begins[0], width)
        weights = [
            [jnp.broadcast_to(fir_ref[tap : tap + 1, pl.ds(begin, width)], (rows, width)) for tap in range(taps)]
            for begin in begins
        ]

        def step(spec, past):
            now = [volt_ref[:, pl.ds(pl.multiple_of(spec * frame + begin, width), width)] for begin in begins]
            sides = [weighted((now[k],) + past[k], weights[k]) for k in range(2)]
            block, group = lax.rem(spec, blocks), lax.div(spec, blocks)
            for ref, value in zip(out_refs, folded(*sides)):
                ref[block, group, :, here] = value
            return tuple((now[k],) + past[k][:-1] for k in range(2))

        past = tuple(
            tuple(
                halo_ref[:, pl.ds(pl.multiple_of((edge - 1 - k) * frame + begin, width), width)]
                for k in range(edge)
            )
            for begin in begins
        )
        lax.fori_loop(0, blocks * groups, step, past, unroll=4)
        return carry

    lax.fori_loop(0, frame // 2 // width, columns, 0)


def filtered_parts(voltages, halo, fir_taps, blocks, groups):
    inputs, samples = voltages.shape
    taps, frame = fir_taps.shape
    rows = 16
    shape = jax.ShapeDtypeStruct((blocks, groups, inputs, frame // 2), jnp.bfloat16)
    out_spec = pl.BlockSpec((blocks, groups, rows, frame // 2), lambda g: (0, 0, g, 0))
    made = pl.pallas_call(
        functools.partial(filter_kernel, blocks, groups, taps),
        grid=(inputs // rows,),
        in_specs=[
            pl.BlockSpec((rows, samples), lambda g: (g, 0)),
            pl.BlockSpec((rows, halo.shape[1]), lambda g: (g, 0)),
            pl.BlockSpec((taps, frame), lambda g: (0, 0)),
        ],
        out_specs=[out_spec] * 4,
        out_shape=[shape] * 4,
        compiler_params=params(60),
        cost_estimate=pl.CostEstimate(
            flops=8000 * inputs * samples, bytes_accessed=8 * inputs * samples, transcendentals=0
        ),
        name="polyphase_filter",
    )(voltages, halo, fir_taps)
    made = [part.reshape(blocks * groups * inputs, frame // 2) for part in made]
    return made[:2], made[2:]


def fill_table(owners, per, outer_ref, first_ref, second_ref, high_ref, low_ref):
    many = 16 // math.gcd(per, 16)

    def rows(step, carry):
        parts = []
        for extra in range(many):
            owner = step * many + extra
            cosine = outer_ref[0, pl.ds(owner, 1), :]
            sine = outer_ref[1, pl.ds(owner, 1), :]
            parts.append(first_ref[...] * cosine + second_ref[...] * sine)
        value = parts[0] if many == 1 else jnp.concatenate(parts, axis=0)
        high, low = halves(value)
        at = pl.ds(pl.multiple_of(step * many * per, many * per), many * per)
        high_ref[at, :] = high
        low_ref[at, :] = low
        return carry

    lax.fori_loop(0, owners // many, rows, 0)


def transform(owners, per, table_high, table_low, high, low, out_ref):
    dot = functools.partial(lax.dot_general, dimension_numbers=NT, preferred_element_type=jnp.float32)
    total = dot(table_high[...], high) + dot(table_high[...], low) + dot(table_low[...], high)
    for block in range(high.shape[0] // LANES):
        part = total[:, block * LANES : (block + 1) * LANES]
        out_ref[:, block * per : (block + 1) * per, :] = part.reshape(owners, per, LANES)


def dft_kernel(owners, per, outer_ref, first_ref, second_ref, high_ref, low_ref, *rest):
    out_ref, th_ref, tl_ref = rest[-3:]

    @pl.when(pl.program_id(0) == 0)
    def _():
        fill_table(owners, per, outer_ref, first_ref, second_ref, th_ref, tl_ref)

    transform(owners, per, th_ref, tl_ref, high_ref[...], low_ref[...], out_ref)


def dft_chunk(outer, first, second, high, low, blocks, held, base, total_rows, token=None):
    per, frame = first.shape
    owners = outer.shape[1]
    wide = 2 * WIDE if blocks % (2 * WIDE) == 0 and base % (2 * WIDE * per) == 0 else WIDE
    rows = wide * LANES
    assert base % (wide * per) == 0
    skip = base // (wide * per)
    const = lambda b: (0, 0)
    operands = [outer, first, second, high, low]
    in_specs = [
        pl.BlockSpec((2, owners, frame), lambda b: (0, 0, 0)),
        pl.BlockSpec((per, frame), const),
        pl.BlockSpec((per, frame), const),
        pl.BlockSpec((rows, frame), lambda b: (b, 0)),
        pl.BlockSpec((rows, frame), lambda b: (b, 0)),
    ]
    aliases = {}
    if held is not None:
        operands.append(held)
        in_specs.append(pl.BlockSpec(memory_space=pl.ANY))
        aliases = {5: 0}
    if token is not None:
        operands.append(token)
        in_specs.append(pl.BlockSpec(memory_space=pl.ANY))
    return pl.pallas_call(
        functools.partial(dft_kernel, owners, per),
        grid=(blocks // wide,),
        in_specs=in_specs,
        out_specs=pl.BlockSpec((owners, wide * per, LANES), lambda b: (0, skip + b, 0)),
        out_shape=jax.ShapeDtypeStruct((owners, total_rows, LANES), jnp.float32),
        input_output_aliases=aliases,
        scratch_shapes=[
            pltpu.VMEM((owners * per, frame), jnp.bfloat16),
            pltpu.VMEM((owners * per, frame), jnp.bfloat16),
        ],
        compiler_params=params(60),
        cost_estimate=pl.CostEstimate(
            flops=60 * owners * per * frame * blocks * LANES,
            bytes_accessed=4 * blocks * LANES * frame + 4 * owners * blocks * per * LANES,
            transcendentals=0,
        ),
        name="dft_chunk",
    )(*operands)


def first_kernel(owners, per, taps, groups, *refs):
    now = refs[:groups]
    fir_ref, outer_ref, first_ref, second_ref, out_ref = refs[groups : groups + 5]
    th_ref, tl_ref, past_ref, high_ref, low_ref = refs[groups + 5 :]
    inputs = now[0].shape[0]
    frame = fir_ref.shape[1]
    edge = taps - 1
    pair = pl.program_id(0)
    ahead = pl.cdiv(edge, WIDE)

    @pl.when(pair == 0)
    def _():
        fill_table(owners, per, outer_ref, first_ref, second_ref, th_ref, tl_ref)

    @pl.when(pair < ahead)
    def _():
        @pl.when(pair > 0)
        def _():
            for k in range(edge - WIDE):
                past_ref[k] = past_ref[k + WIDE]

        for group in range(groups):
            for k in range(WIDE):
                past_ref[edge - WIDE + k, group] = now[group][:, k * frame : (k + 1) * frame]

    @pl.when(pair >= ahead)
    def _():
        rows = 16
        width = 2 * LANES

        def columns(column, carry):
            begins = [
                pl.multiple_of(column * width, width),
                pl.multiple_of(column * width + frame // 2, width),
            ]
            weights = [
                [
                    jnp.broadcast_to(fir_ref[tap : tap + 1, pl.ds(begin, width)], (rows, width))
                    for tap in range(taps)
                ]
                for begin in begins
            ]
            for group in range(groups):
                for start in range(0, inputs, rows):
                    at = pl.ds(start, rows)
                    sums = [None] * WIDE
                    for begin, weight in zip(begins, weights):
                        here = pl.ds(begin, width)
                        frames = [past_ref[k, group, at, here] for k in range(edge)]
                        for spec in range(WIDE):
                            frames.append(
                                now[group][at, pl.ds(pl.multiple_of(spec * frame + begin, width), width)]
                            )
                        for spec in range(WIDE):
                            total = weighted([frames[edge + spec - tap] for tap in range(taps)], weight)
                            sums[spec] = total if sums[spec] is None else sums[spec] + total
                        for k in range(edge):
                            past_ref[k, group, at, here] = frames[WIDE + k]
                    for spec in range(WIDE):
                        high, low = halves(sums[spec])
                        place = pl.ds(spec * LANES + group * inputs + start, rows)
                        high_ref[place, pl.ds(begins[0], width)] = high
                        low_ref[place, pl.ds(begins[0], width)] = low
            return carry

        lax.fori_loop(0, frame // 2 // width, columns, 0)
        transform(owners, per, th_ref, tl_ref, high_ref[...], low_ref[...], out_ref)


def first_chunk(outer, first, second, voltages, fir_taps, blocks, groups):
    per, half = first.shape
    owners = outer.shape[1]
    inputs, samples = voltages.shape
    taps, frame = fir_taps.shape
    kept = blocks - LATE
    const = lambda b: (0, 0)

    ahead = pl.cdiv(taps - 1, WIDE)

    def now_map(group):
        return lambda b: (0, (group * blocks + LATE) // WIDE - ahead + b)

    return pl.pallas_call(
        functools.partial(first_kernel, owners, per, taps, groups),
        grid=(kept // WIDE + ahead,),
        in_specs=[pl.BlockSpec((inputs, WIDE * frame), now_map(g)) for g in range(groups)]
        + [
            pl.BlockSpec((taps, frame), const),
            pl.BlockSpec((2, owners, half), lambda b: (0, 0, 0)),
            pl.BlockSpec((per, half), const),
            pl.BlockSpec((per, half), const),
        ],
        out_specs=pl.BlockSpec((owners, WIDE * per, LANES), lambda b: (0, jnp.maximum(b - ahead, 0), 0)),
        out_shape=jax.ShapeDtypeStruct((owners, kept * per, LANES), jnp.float32),
        scratch_shapes=[
            pltpu.VMEM((owners * per, half), jnp.bfloat16),
            pltpu.VMEM((owners * per, half), jnp.bfloat16),
            pltpu.VMEM((taps - 1, groups, inputs, frame), jnp.float32),
            pltpu.VMEM((WIDE * LANES, half), jnp.bfloat16),
            pltpu.VMEM((WIDE * LANES, half), jnp.bfloat16),
        ],
        compiler_params=params(60),
        cost_estimate=pl.CostEstimate(
            flops=6 * owners * per * half * kept * LANES,
            bytes_accessed=4 * inputs * samples,
            transcendentals=0,
        ),
        name="first_chunk",
    )(*([voltages] * groups), fir_taps, outer, first, second)


def correlate_kernel(sizes, places, *refs):
    tm_count, chan_count, blocks, per, inputs = sizes
    groups = LANES // inputs
    channels = per // 2
    if places is None:
        got_ref, (out_ref, token_ref) = refs[0], refs[-2:]
    else:
        out_ref, token_ref, got_ref, sems = refs[-4:]

    @pl.when(pl.program_id(0) == 0)
    def _():
        token_ref[...] = jnp.zeros_like(token_ref)

    @pl.when(pl.program_id(0) == 0)
    def _():
        copies = []
        for index, (base, rows, into) in enumerate(places or []):
            source = refs[index].at[:, pl.ds(base, rows), :]
            target = got_ref.at[:, pl.ds(into, rows), :]
            copies.append(pltpu.make_async_copy(source, target, sems.at[index]))
            copies[-1].start()
        for copy in copies:
            copy.wait()

    lane_group = lax.broadcasted_iota(jnp.int32, (blocks, LANES), 1) // inputs

    def piece(channel, time, chan, part):
        rows = pl.ds(part * channels + channel, blocks, stride=per)
        return got_ref[time * chan_count + chan, rows, :]

    def tile(channel, time, part, column):
        held = [piece(channel, time, column * groups + place, part) for place in range(groups)]
        made = []
        for group in range(groups):
            total = None
            for place in range(groups):
                turn = (place - group) * inputs % LANES
                value = pltpu.roll(held[place], turn, 1) if turn else held[place]
                total = value if total is None else jnp.where(lane_group == place, value, total)
            made.append(total)
        return jnp.concatenate(made, axis=0)

    def plane(channel, part):
        columns = []
        for column in range(chan_count // groups):
            columns.append(
                jnp.concatenate([tile(channel, time, part, column) for time in range(tm_count)], axis=0)
            )
        return jnp.concatenate(columns, axis=1)

    dot = functools.partial(lax.dot_general, dimension_numbers=NN, preferred_element_type=jnp.float32)
    for sub in range(PAIR):
        channel = pl.program_id(0) * PAIR + sub
        real, imag = plane(channel, 0), plane(channel, 1)
        real_high, real_low = halves(real)
        imag_high, imag_low = halves(imag)
        high = jnp.concatenate([real_high, imag_high], axis=0)
        low = jnp.concatenate([real_low, imag_low], axis=0)
        turned_high = jnp.concatenate([-imag_high, real_high], axis=0)
        turned_low = jnp.concatenate([-imag_low, real_low], axis=0)
        high_t, low_t = high.T, low.T
        for which, (other_high, other_low) in enumerate([(high, low), (turned_high, turned_low)]):
            total = dot(high_t, other_high) + dot(high_t, other_low) + dot(low_t, other_high)
            out_ref[sub, 0, which] = total


def correlate_chunk(pieces, held, start, owned, sizes, spectra):
    tm_count, chan_count, blocks, per, inputs = sizes
    channels = per // 2
    everyone = chan_count * inputs
    owners = tm_count * chan_count
    operands = [piece[0] for piece in pieces]
    places = [piece[1:] for piece in pieces]
    in_specs = [pl.BlockSpec(memory_space=pl.ANY)] * len(operands)
    limit = 60
    scratch = [
        pltpu.VMEM((owners, blocks * per, LANES), jnp.float32),
        pltpu.SemaphoreType.DMA((len(pieces),)),
    ]
    if len(pieces) == 1 and operands[0].shape[1] == blocks * per and per <= 8:
        places, scratch, limit = None, [], 40
        in_specs = [pl.BlockSpec(operands[0].shape, lambda c: (0, 0, 0))]
    aliases = {}
    if held is not None:
        aliases = {len(operands): 0}
        operands.append(held)
        in_specs.append(pl.BlockSpec(memory_space=pl.ANY))
    return pl.pallas_call(
        functools.partial(correlate_kernel, sizes, places),
        grid=(channels // PAIR,),
        in_specs=in_specs,
        out_specs=[
            pl.BlockSpec((PAIR, 1, 2, everyone, everyone), lambda c: (start // 2 // PAIR + c, start % 2, 0, 0, 0)),
            pl.BlockSpec((8, LANES), lambda c: (0, 0)),
        ],
        out_shape=[
            jax.ShapeDtypeStruct((owned // 2, 2, 2, everyone, everyone), jnp.float32),
            jax.ShapeDtypeStruct((8, LANES), jnp.float32),
        ],
        input_output_aliases=aliases,
        scratch_shapes=scratch,
        compiler_params=params(limit),
        cost_estimate=pl.CostEstimate(
            flops=6 * channels * 2 * everyone * everyone * 2 * spectra,
            bytes_accessed=channels * 8 * everyone * everyone + 4 * owners * blocks * per * LANES,
            transcendentals=0,
        ),
        name="correlate_chunk",
    )(*operands)


def chunk_plan(owned):
    unit = owned // 8
    if owned % 32 == 0:
        return [[(0, 4 * unit)], [(2 * unit + 1, 3 * unit)], [(1, unit)]]
    return [[(parity, owned // 2)] for parity in (0, 1)]


def phases(frame, owners, owned, segments, spectra):
    samples = np.arange(frame // 2)
    outer = 2.0 * np.pi * ((np.arange(owners)[:, None] * owned * samples) % frame) / frame
    outer = np.stack([np.cos(outer), np.sin(outer)]).astype(np.float32)
    scale = 1.0 / np.sqrt(float(frame * spectra))
    tables = {}
    for start, count in segments:
        channels = start + 2 * np.arange(count)
        inner = 2.0 * np.pi * ((channels[:, None] * samples) % frame) / frame
        cosine, sine = np.cos(inner) * scale, np.sin(inner) * scale
        first = np.concatenate([cosine, -sine]).astype(np.float32)
        second = np.concatenate([-sine, -cosine]).astype(np.float32)
        tables[start, count] = (first, second)
    return outer, tables


def body(voltages, fir_taps):
    inputs, samples = voltages.shape
    taps, frame = fir_taps.shape
    spec_dev = samples // frame
    tm_count, chan_count = lax.axis_size("tm"), lax.axis_size("chan")
    owners = tm_count * chan_count
    owned = frame // 2 // owners
    groups = LANES // inputs
    blocks = spec_dev // groups
    chunks = chunk_plan(owned)
    outer, tables = phases(frame, owners, owned, sum(chunks, []), tm_count * spec_dev)
    split = blocks > LATE and len(chunks) > 2

    def exchange(value):
        return lax.all_to_all(value, AXES, split_axis=0, concat_axis=0, tiled=True)

    halo = passed_along(voltages[:, samples - (taps - 1) * frame :], "tm", 1)
    if split:
        ahead = first_chunk(outer, *tables[chunks[0][0]], voltages, fir_taps, blocks, groups)
    parts = filtered_parts(voltages, halo, fir_taps, blocks, groups)

    def transformed(segment, count, made, base, rows, token):
        return dft_chunk(
            outer, *tables[segment], *parts[segment[0] % 2], count, made, base, rows, token
        )

    pieces = {segment: [] for segment in sum(chunks, [])}
    out, token = None, None

    def correlate(segments):
        nonlocal out, token
        for segment in segments:
            start, count = segment
            sizes = (tm_count, chan_count, blocks, 2 * count, inputs)
            out, token = correlate_chunk(
                pieces[segment], out, start, owned, sizes, tm_count * spec_dev
            )

    payloads, layouts = [], []
    for index, chunk in enumerate(chunks):
        if index == 0 and split:
            (segment,) = chunk
            per = 2 * segment[1]
            pieces[segment].append((exchange(ahead), 0, (blocks - LATE) * per, LATE * per))
            continue
        plan = [(segment, blocks) for segment in chunk]
        if index == 1 and split:
            plan.append((chunks[0][0], LATE))
        rows = sum(2 * segment[1] * count for segment, count in plan)
        made, base, places = None, 0, []
        for segment, count in plan:
            made = transformed(segment, count, made, base, rows, token)
            places.append((segment, base, 2 * segment[1] * count))
            base += 2 * segment[1] * count
        payloads.append(made)
        layouts.append(places)
    payloads = lax.optimization_barrier(tuple(payloads))
    for made, places in zip(payloads, layouts):
        got = exchange(made)
        for segment, base, more in places:
            pieces[segment].append((got, base, more, 0))
    correlate(sum(chunks, []))
    return out.reshape(owned, 2, chan_count * inputs, chan_count * inputs)


def solution(mesh):
    placed = (P("chan", "tm"), P())
    return jax.shard_map(
        body,
        mesh=mesh,
        in_specs=placed,
        out_specs=P(("tm", "chan"), None, None, None),
        check_vma=False,
    )
```
